128 devices in a mesh: segment: 4 (over z), seq: 32 (over x, y, core).
Axes of the slice: x: 4, y: 4, z: 4, core: 2. Of those that a mesh axis runs over, the one named last changes fastest.
Arguments:
- queries: bfloat16 [4, 16384, 8192], P('segment', 'seq'), may hold values from -40 to 40
- keys_in: bfloat16 [4, 16384, 1024], P('segment', 'seq'), may hold values from -6 to 6
- values_in: bfloat16 [4, 16384, 1024], P('segment', 'seq'), may hold values from -6 to 6
- random_blocks: int32 [4, 256, 3], P('segment', 'seq'), may hold values from 0 to 255, as said below
- global_blocks: int32 [4, 2], P('segment'), may hold values from 0 to 255
Outputs:
- handed: bfloat16 [4, 16384, 8192], P('segment', 'seq')
The draws below stay inside these ranges and needn't reach their ends.
Inputs may be any that keep to these rules, and one draw needn't show every extreme that they name: random_blocks[s, j] are block numbers; the rows of one device of seq name at most 1 block lying on any single device of seq, and in every section one device of seq is named exactly once by the rows of every device.
All inputs are finite; a program needn't handle non-finite values.
Results may differ from the reference program's by a relative error of at most 0.0049.
Values may be sent and summed in bfloat16 or wider, within the bound.
No kernel may reach another device: no remote copies, remote signals or barrier semaphores. Data moves between devices by JAX's collectives and lax.ppermute only.
A program may use at most 128 MiB of HBM per device.

```python
import jax
import jax.numpy as jnp
from jax import lax

HEADS = 64
KV_HEADS = 8
HEAD = 128
BLOCK = 64
GLOB = 2
RAND = 3
TOK_DEV = 512
SEGMENTS = 4
TOKENS = 16384
BLK_DEV = 8
NBLK = 256
CAP = 1
KEYS = 512


def shared_noise(key):
    shape = (SEGMENTS, TOKENS, KV_HEADS * HEAD)
    gauss = jax.random.normal(jax.random.fold_in(key, 101), shape, jnp.float32)
    return gauss


def draw_keys_in(key, part):
    gauss = shared_noise(key)
    key_rows = jnp.clip(gauss, -6.0, 6.0)
    return key_rows.astype(jnp.bfloat16)


def draw_queries(key, part):
    key = jax.random.fold_in(key, 2)
    shape = (SEGMENTS, TOKENS, HEADS * HEAD)
    result = jnp.clip(2.0 * jax.random.normal(key, shape, jnp.float32), -8.0, 8.0)
    return result.astype(jnp.bfloat16)


def draw_random_blocks(key, part):
    key = jax.random.fold_in(key, 5)
    number_of_strings = TOKENS // TOK_DEV
    wanted = BLK_DEV * RAND
    tile_locations = number_of_strings * CAP
    holder_processor = jnp.arange(tile_locations, dtype=jnp.int32) // CAP
    sorted_ordinals = jnp.arange(tile_locations, dtype=jnp.int32)

    def one_segment(segment_key):
        foremost_tile, second, third = jax.random.split(segment_key, 3)
        preference_increment = jax.random.randint(foremost_tile, (number_of_strings,), 0, 4)
        picked_tile_flags = jax.random.randint(second, (), 0, number_of_strings)

        def one_device(device_key):
            noise_key, shuffle_key, local_key = jax.random.split(device_key, 3)
            stochastic_perturbation = jax.random.randint(noise_key, (tile_locations,), 0, 16384)
            raw_affinity_table = (preference_increment[holder_processor] * 16384 + stochastic_perturbation + jnp.where(holder_processor == picked_tile_flags, 131072, 0)) * tile_locations + sorted_ordinals
            chosen = lax.top_k(raw_affinity_table, wanted)[1]
            owners = jax.random.permutation(shuffle_key, holder_processor[chosen])
            local = jax.random.randint(local_key, (wanted,), 0, BLK_DEV)
            return (owners * BLK_DEV + local).reshape(BLK_DEV, RAND)
        per_device = jax.vmap(one_device)(jax.random.split(third, number_of_strings))
        return per_device.reshape(NBLK, RAND)
    return jax.vmap(one_segment)(jax.random.split(key, SEGMENTS)).astype(jnp.int32)


def with_ends(drawn, key, least, largest):
    longest = drawn.shape.index(max(drawn.shape))
    spots = []
    for shift in (0, 1):
        where = [jax.random.randint(jax.random.fold_in(key, axis), (), 0, length) for axis, length in enumerate(drawn.shape)]
        where[longest] = (where[longest] + shift) % drawn.shape[longest]
        spots.append(tuple(where))
    return drawn.at[spots[0]].set(least).at[spots[1]].set(largest)


def shard_levels(rng, shape, cuts, least, largest):
    factor_of = 1.0
    for axis_at, shards_of in cuts:
        heights = jax.random.uniform(jax.random.fold_in(jax.random.fold_in(rng, 6), axis_at), (shards_of,), jnp.float32, least / len(cuts), largest / len(cuts))
        factor_of = factor_of * jnp.repeat(jnp.exp(heights), shape[axis_at] // shards_of).reshape((-1,) + (1,) * (len(shape) - 1 - axis_at))
    return factor_of


def normal_values(key, dims, spread, reach, shards=(), kind=jnp.bfloat16):
    values = jax.random.normal(key, dims, jnp.float32) * spread
    if len(shards) > 0:
        values = shard_levels(key, dims, shards, -0.22, 0.18) * values
    return jnp.clip(values, min=-reach, max=reach).astype(kind)


def setup_inputs(seed: int = 0) -> dict:
    keys = jax.random.split(jax.random.key(seed), 6)
    return {
        "queries": draw_queries(jax.random.fold_in(keys[5], 71), 0),
        "keys_in": draw_keys_in(jax.random.fold_in(keys[5], 71), 0),
        "values_in": normal_values(keys[2], (SEGMENTS, TOKENS, KV_HEADS * HEAD), 1.0, 6.0, ((0, 4), (1, 32))),
        "random_blocks": draw_random_blocks(jax.random.fold_in(keys[5], 71), 0),
        "global_blocks": with_ends(jax.random.randint(keys[4], (SEGMENTS, GLOB), 0, NBLK), jax.random.fold_in(keys[4], 1), 0, NBLK - 1).astype(jnp.int32),
    }


def attend(query_rows, key_rows, value_rows, random_rows, global_row):
    nblk = query_rows.shape[0] // BLOCK
    kvw = key_rows.shape[1]
    group = HEADS // KV_HEADS
    stacked = jnp.concatenate([key_rows, value_rows], axis=-1).reshape(nblk, BLOCK, 2 * kvw)
    query_blocks = query_rows.reshape(nblk, BLOCK, KV_HEADS, group, HEAD)
    scale = 1.0 / (HEAD ** 0.5)

    def one_row(j):
        listed = jnp.concatenate([j + jnp.array([-1, 0, 1], jnp.int32), global_row, random_rows[j]]).astype(jnp.int32)
        valid = jnp.concatenate([jnp.stack([j >= 1, j >= 0, j + 1 < nblk]), jnp.ones((GLOB + RAND,), bool)])
        picked = stacked[jnp.clip(listed, 0, nblk - 1)].reshape(KEYS, 2 * kvw)
        key_portion = picked[:, :kvw].reshape(KEYS, KV_HEADS, HEAD).astype(jnp.float32)
        value_portion = picked[:, kvw:].reshape(KEYS, KV_HEADS, HEAD).astype(jnp.float32)
        query_portion = query_blocks[j].astype(jnp.float32)
        scores = jnp.einsum('qhgd,khd->hgqk', query_portion, key_portion) * scale
        mask = jnp.repeat(valid, BLOCK)
        scores = jnp.where(mask[None, None, None, :], scores, -jnp.inf)
        top = jnp.max(scores, axis=-1, keepdims=True)
        expo = jnp.exp(scores - top)
        attention_probs = (expo / jnp.sum(expo, axis=-1, keepdims=True)).astype(jnp.bfloat16)
        attention_probs = lax.optimization_barrier(attention_probs).astype(jnp.float32)
        result = jnp.einsum('hgqk,khd->qhgd', attention_probs, value_portion)
        return result.astype(jnp.bfloat16).reshape(BLOCK, HEADS * HEAD)

    rows = lax.map(one_row, jnp.arange(nblk, dtype=jnp.int32))
    return rows.reshape(nblk * BLOCK, HEADS * HEAD)


def reference(queries, keys_in, values_in, random_blocks, global_blocks):
    sections = []
    for section in range(queries.shape[0]):
        sections.append(attend(queries[section], keys_in[section], values_in[section], random_blocks[section], global_blocks[section]))
    attended = jnp.stack(sections)
    return jnp.roll(attended, 1, axis=0)
```

```python
import math

import jax
import jax.numpy as jnp
from jax import lax
from jax.experimental import pallas as pl
from jax.experimental.pallas import tpu as pltpu
from jax.sharding import PartitionSpec as P

HEAD = 128
BLOCK = 64
GLOB = 2
RAND = 3
ROWS = 512
BLOCKS = ROWS // BLOCK
GROUP = 8
PAIR = 2
TILES = 2 * PAIR
CHUNKS = 4
DEVS = 32
PIECE = 16
KEYS = 512
SLOT = TILES * BLOCK + PIECE
QW = GROUP * HEAD
BF = jnp.bfloat16
SCALE = math.log2(math.e) / math.sqrt(HEAD)
VMEM_BYTES = 48 << 20


def along(x, axis, by):
    n = lax.axis_size(axis)
    return lax.ppermute(x, axis, [(i, (i + by) % n) for i in range(n)])


def exchange(x):
    return lax.all_to_all(x, "seq", split_axis=0, concat_axis=0, tiled=True)


def params():
    return pltpu.CompilerParams(vmem_limit_bytes=VMEM_BYTES)


def first_message(owners, local, near, keys, values):
    def body(own, loc, near_ref, k0, k1, v0, v1, out):
        for i in range(DEVS):
            g, t, part = i // 16, (i % 16) // 4, i % 4
            src = ((k0, k1), (v0, v1))[t // PAIR][g]
            for c in range(CHUNKS):
                head = PAIR * c + t % PAIR
                out[i, c * PIECE : (c + 1) * PIECE] = src[
                    part * PIECE : (part + 1) * PIECE, head * HEAD : (head + 1) * HEAD
                ]
        out[:, CHUNKS * PIECE :] = jnp.zeros((DEVS, PIECE, HEAD), BF)
        for r in range(BLOCKS * RAND):
            out[own[r], CHUNKS * PIECE :] = jnp.full((PIECE, HEAD), loc[r], jnp.int32).astype(
                jnp.float32
            ).astype(BF)

    def spec(g):
        return pl.BlockSpec((BLOCK, keys.shape[1]), lambda i, own, loc, near: (near[g], 0))

    return pl.pallas_call(
        body,
        grid_spec=pltpu.PrefetchScalarGridSpec(
            num_scalar_prefetch=3,
            grid=(1,),
            in_specs=[spec(0), spec(1), spec(0), spec(1)],
            out_specs=pl.BlockSpec((DEVS, (CHUNKS + 1) * PIECE, HEAD), lambda i, *_: (0, 0, 0)),
        ),
        out_shape=jax.ShapeDtypeStruct((DEVS, (CHUNKS + 1) * PIECE, HEAD), BF),
        compiler_params=params(),
    )(owners, local, near, keys, keys, values, values)


def pack(asked, k, k_at, v, v_at, piece):
    step = 8

    def body(ask, k_ref, v_ref, p_ref, out):
        base = pl.program_id(0) * step
        for d in range(step):
            rows = pl.ds(pl.multiple_of(ask[base + d] * BLOCK, BLOCK), BLOCK)
            for t in range(TILES):
                src = (k_ref, v_ref)[t // PAIR]
                at = (t % PAIR) * HEAD
                out[d, t * BLOCK : (t + 1) * BLOCK] = src[rows, at : at + HEAD]
            out[d, TILES * BLOCK :] = p_ref[...]

    return pl.pallas_call(
        body,
        grid_spec=pltpu.PrefetchScalarGridSpec(
            num_scalar_prefetch=1,
            grid=(DEVS // step,),
            in_specs=[
                pl.BlockSpec((ROWS, PAIR * HEAD), lambda i, *_: (0, k_at)),
                pl.BlockSpec((ROWS, PAIR * HEAD), lambda i, *_: (0, v_at)),
                pl.BlockSpec((PIECE, HEAD), lambda i, *_: (0, 0)),
            ],
            out_specs=pl.BlockSpec((step, SLOT, HEAD), lambda i, *_: (i, 0, 0)),
        ),
        out_shape=jax.ShapeDtypeStruct((DEVS, SLOT, HEAD), BF),
        compiler_params=params(),
    )(asked, k, v, piece)


def attention(slots, flags, q, q_at, k, k_at, v, v_at, before, after, hk_at, hv_at, got, out=None, out_at=0, width=None):
    def body(slot, flag, q_ref, k_ref, v_ref, kb, vb, ka, va, rk, rv, gl, *rest):
        o_ref, kpad, vpad, kcat, vcat = rest[-5:]
        h = pl.program_id(0)
        for pad, own, b, a in ((kpad, k_ref, kb, ka), (vpad, v_ref, vb, va)):
            pad[0:BLOCK] = b[...]
            pad[BLOCK : BLOCK + ROWS] = own[...]
            pad[BLOCK + ROWS :] = a[...]
        for buf in range(2):
            for g in range(GLOB):
                for part in range(4):
                    at = 3 * BLOCK + g * BLOCK + part * PIECE
                    kcat[buf, at : at + PIECE] = gl[g * 16 + h * 4 + part]
                    vcat[buf, at : at + PIECE, 0:HEAD] = gl[g * 16 + (PAIR + h) * 4 + part]
            vcat[buf, :, HEAD:] = jnp.ones((KEYS, HEAD), BF)
        for j in range(BLOCKS):
            buf = j % 2
            kcat[buf, 0 : 3 * BLOCK] = kpad[j * BLOCK : (j + 3) * BLOCK]
            vcat[buf, 0 : 3 * BLOCK, 0:HEAD] = vpad[j * BLOCK : (j + 3) * BLOCK]
            for r in range(RAND):
                s = slot[j * RAND + r]
                at = (3 + GLOB + r) * BLOCK
                kcat[buf, at : at + BLOCK] = rk[s]
                vcat[buf, at : at + BLOCK, 0:HEAD] = rv[s]
            rows = slice(j * BLOCK, (j + 1) * BLOCK)
            part_heads = 2
            for u in range(GROUP // part_heads):
                heads = range(u * part_heads, (u + 1) * part_heads)
                qq = jnp.concatenate([q_ref[rows, g * HEAD : (g + 1) * HEAD] for g in heads], axis=0)
                s = lax.dot_general(
                    qq, kcat[buf], (((1,), (1,)), ((), ())), preferred_element_type=jnp.float32
                )
                if j == 0 or j == BLOCKS - 1:
                    col = lax.broadcasted_iota(jnp.int32, (1, KEYS), 1)
                    if j == 0:
                        hide = (col < BLOCK) & (flag[0] == 0)
                    else:
                        hide = (col >= 2 * BLOCK) & (col < 3 * BLOCK) & (flag[1] == 0)
                    s = jnp.where(hide, -jnp.inf, s)
                top = jnp.max(s, axis=-1, keepdims=True)
                e = jnp.exp2((s - top) * SCALE).astype(BF)
                o = lax.dot_general(
                    e, vcat[buf], (((1,), (0,)), ((), ())), preferred_element_type=jnp.float32
                )
                o = (o[:, :HEAD] / o[:, HEAD:]).astype(BF)
                for n, g in enumerate(heads):
                    o_ref[rows, g * HEAD : (g + 1) * HEAD] = o[n * BLOCK : (n + 1) * BLOCK]

    def col(shape, at):
        return pl.BlockSpec(shape, lambda h, *_: (0, at + h))

    in_specs = [
        col((ROWS, QW), q_at),
        col((ROWS, HEAD), k_at),
        col((ROWS, HEAD), v_at),
        col((BLOCK, HEAD), hk_at),
        col((BLOCK, HEAD), hv_at),
        col((BLOCK, HEAD), hk_at),
        col((BLOCK, HEAD), hv_at),
        pl.BlockSpec((DEVS, BLOCK, HEAD), lambda h, *_: (0, h, 0)),
        pl.BlockSpec((DEVS, BLOCK, HEAD), lambda h, *_: (0, PAIR + h, 0)),
        pl.BlockSpec((DEVS, PIECE, HEAD), lambda h, *_: (0, TILES * BLOCK // PIECE, 0)),
    ]
    operands = [slots, flags, q, k, v, before, before, after, after, got, got, got]
    aliases = {}
    if out is not None:
        in_specs.append(pl.BlockSpec(memory_space=pl.ANY))
        aliases = {len(operands): 0}
        operands.append(out)
    return pl.pallas_call(
        body,
        grid_spec=pltpu.PrefetchScalarGridSpec(
            num_scalar_prefetch=2,
            grid=(PAIR,),
            in_specs=in_specs,
            out_specs=pl.BlockSpec((ROWS, QW), lambda h, *_: (0, out_at + h)),
            scratch_shapes=[
                pltpu.VMEM((ROWS + 2 * BLOCK, HEAD), BF),
                pltpu.VMEM((ROWS + 2 * BLOCK, HEAD), BF),
                pltpu.VMEM((2, KEYS, HEAD), BF),
                pltpu.VMEM((2, KEYS, 2 * HEAD), BF),
            ],
        ),
        out_shape=jax.ShapeDtypeStruct((ROWS, width or PAIR * QW), BF),
        input_output_aliases=aliases,
        compiler_params=params(),
    )(*operands)


def place(part, out, at):
    step = ROWS // 4

    def body(p_ref, _, o_ref):
        o_ref[...] = p_ref[...]

    return pl.pallas_call(
        body,
        grid=(4,),
        in_specs=[
            pl.BlockSpec((step, part.shape[1]), lambda i: (i, 0)),
            pl.BlockSpec(memory_space=pl.ANY),
        ],
        out_specs=pl.BlockSpec((step, part.shape[1]), lambda i: (i, at)),
        out_shape=jax.ShapeDtypeStruct(out.shape, BF),
        input_output_aliases={1: 0},
        compiler_params=params(),
    )(part, out)


def per_device(queries, keys_in, values_in, random_blocks, global_blocks):
    q, keys, values = queries[0], keys_in[0], values_in[0]
    me = lax.axis_index("seq")
    half = 2 * PAIR * HEAD

    near_q = along(q[:, 2 * PAIR * QW : 3 * PAIR * QW], "segment", 1)
    far_q = q[:, 3 * PAIR * QW :]
    for _ in range(lax.axis_size("segment") - 1):
        far_q = along(far_q, "segment", -1)

    wanted = random_blocks[0].reshape(BLOCKS * RAND)
    owners = wanted // BLOCKS
    near = jnp.clip(global_blocks[0] - me * BLOCKS, 0, BLOCKS - 1)
    message = exchange(first_message(owners, wanted % BLOCKS, near, keys, values))
    asked = message[:, CHUNKS * PIECE, 0].astype(jnp.int32)
    holder = global_blocks[0] // BLOCKS
    pieces = lax.dynamic_index_in_dim(
        message, jnp.where(me < DEVS // GLOB, holder[0], holder[1]), axis=0, keepdims=False
    )
    flags = jnp.stack([me > 0, me < DEVS - 1]).astype(jnp.int32)

    def piece(c):
        return pieces[c * PIECE : (c + 1) * PIECE]

    low = jnp.concatenate([keys[:, :half], values[:, :half]], axis=1)
    before = along(low[ROWS - BLOCK :], "seq", 1)
    after = along(low[:BLOCK], "seq", -1)

    got = []
    for c in range(2):
        got.append(exchange(pack(asked, keys, c, values, c, piece(c))))

    notes = jnp.concatenate([asked, owners, jnp.zeros((HEAD - 56,), jnp.int32)]).astype(BF)
    tail = jnp.concatenate(
        [
            piece(2),
            piece(3),
            jnp.broadcast_to(notes[None], (PIECE, HEAD)),
            jnp.zeros((PIECE, 5 * HEAD), BF),
        ],
        axis=1,
    )
    high = jnp.concatenate([keys[:, half:], values[:, half:]], axis=1)
    moved = along(jnp.concatenate([high, tail], axis=0), "segment", 1)
    notes_e = moved[ROWS, 2 * HEAD : 3 * HEAD].astype(jnp.int32)
    asked_e, owners_e = notes_e[:DEVS], notes_e[DEVS : DEVS + BLOCKS * RAND]
    before_e = along(moved[ROWS - BLOCK : ROWS], "seq", 1)
    after_e = along(moved[:BLOCK], "seq", -1)

    sent = []
    for c in range(2):
        res = attention(
            owners, flags, q, PAIR * c, keys, PAIR * c, values, PAIR * c,
            before, after, PAIR * c, 2 * PAIR + PAIR * c, got[c],
        )
        sent.append(along(res, "segment", 1))

    out = None
    for c in range(2):
        packed = pack(asked_e, moved, c, moved, 2 + c, moved[ROWS:, c * HEAD : (c + 1) * HEAD])
        got_e = exchange(packed)
        out = attention(
            owners_e, flags, (near_q, far_q)[c], 0, moved, PAIR * c, moved, 2 * PAIR + PAIR * c,
            before_e, after_e, PAIR * c, 2 * PAIR + PAIR * c, got_e,
            out=out, out_at=2 * PAIR + PAIR * c, width=q.shape[1],
        )
    for c in range(2):
        out = place(sent[c], out, c)
    return out[None]


def solution(mesh):
    in_specs = (
        P("segment", "seq", None),
        P("segment", "seq", None),
        P("segment", "seq", None),
        P("segment", "seq", None),
        P("segment", None),
    )
    out_specs = P("segment", "seq", None)
    return jax.shard_map(
        per_device, mesh=mesh, in_specs=in_specs, out_specs=out_specs, check_vma=False
    )
```

```python
import math

import jax
import jax.numpy as jnp
from jax import lax
from jax.experimental import pallas as pl
from jax.experimental.pallas import tpu as pltpu
from jax.sharding import PartitionSpec as P

HEAD = 128
BLOCK = 64
GLOB = 2
RAND = 3
ROWS = 512
BLOCKS = ROWS // BLOCK
GROUP = 8
HEADS_KV = 8
PAIRS = HEADS_KV // 2
LATE = 3
FAR = 2
DEVS = 32
PIECE = 16
KEYS = 512
WEIGHT = 20
QW = GROUP * HEAD
BF = jnp.bfloat16
SCALE = math.log2(math.e) / math.sqrt(HEAD)
VMEM_BYTES = 63 << 20
CHEAP = pl.CostEstimate(flops=0, bytes_accessed=0, transcendentals=0)


def attention_cost(heads):
    scores = heads * GROUP * ROWS * KEYS
    return pl.CostEstimate(
        flops=WEIGHT * 4 * scores * HEAD, bytes_accessed=WEIGHT * 4 * heads * ROWS * QW, transcendentals=scores
    )


def along(x, axis, by):
    n = lax.axis_size(axis)
    return lax.ppermute(x, axis, [(i, (i + by) % n) for i in range(n)])


def exchange(x):
    return lax.all_to_all(x, "seq", split_axis=0, concat_axis=0, tiled=True)


def params():
    return pltpu.CompilerParams(vmem_limit_bytes=VMEM_BYTES)


def opening(random_blocks, global_blocks, q, keys, values):
    cut = LATE * HEAD
    rest = keys.shape[1] - cut
    message_shape = (DEVS, (PAIRS + 1) * PIECE, HEAD)
    shapes = [message_shape, (ROWS, 2 * rest), (ROWS, QW)]

    def body(rb, gb, q_ref, k_ref, v_ref, out_hbm, high_hbm, far_hbm, out, high, far, glob, sems, glob_sems):
        base = lax.axis_index("seq") * BLOCKS
        globs = []
        for g in range(GLOB):
            at = jnp.minimum(jnp.maximum(gb[g] - base, 0), BLOCKS - 1) * BLOCK
            rows = pl.ds(pl.multiple_of(at, BLOCK), BLOCK)
            for n, src in enumerate((k_ref, v_ref)):
                globs.append(pltpu.make_async_copy(src.at[rows], glob.at[n, g], glob_sems.at[2 * n + g]))
        loads = [
            pltpu.make_async_copy(k_ref.at[:, pl.ds(cut, rest)], high.at[:, pl.ds(0, rest)], sems.at[0]),
            pltpu.make_async_copy(v_ref.at[:, pl.ds(cut, rest)], high.at[:, pl.ds(rest, rest)], sems.at[1]),
            pltpu.make_async_copy(q_ref.at[:, pl.ds((HEADS_KV - FAR) * QW, QW)], far, sems.at[2]),
        ]
        stores = [
            pltpu.make_async_copy(high, high_hbm, sems.at[3]),
            pltpu.make_async_copy(far, far_hbm, sems.at[4]),
            pltpu.make_async_copy(out, out_hbm, sems.at[5]),
        ]
        for c in loads + globs:
            c.start()
        out[:, PAIRS * PIECE :] = jnp.zeros((DEVS, PIECE, HEAD), BF)
        for r in range(RAND):
            for j in range(BLOCKS):
                wanted = rb[r, j]
                out[lax.shift_right_logical(wanted, 3), PAIRS * PIECE :] = jnp.full(
                    (PIECE, HEAD), wanted & (BLOCKS - 1), jnp.int32
                ).astype(jnp.float32).astype(BF)
        loads[0].wait()
        loads[1].wait()
        stores[0].start()
        loads[2].wait()
        stores[1].start()
        for c in globs:
            c.wait()
        for i in range(DEVS):
            g, t, part = i // 16, (i % 16) // 4, i % 4
            for c in range(PAIRS):
                head = 2 * c + t % 2
                out[i, c * PIECE : (c + 1) * PIECE] = glob[
                    t // 2, g, part * PIECE : (part + 1) * PIECE, head * HEAD : (head + 1) * HEAD
                ]
        stores[2].start()
        for c in stores:
            c.wait()

    here = pl.BlockSpec(memory_space=pltpu.HBM)
    return pl.pallas_call(
        body,
        grid_spec=pltpu.PrefetchScalarGridSpec(
            num_scalar_prefetch=2,
            grid=(1,),
            in_specs=[here] * 3,
            out_specs=[here] * 3,
            scratch_shapes=[pltpu.VMEM(x, BF) for x in shapes]
            + [
                pltpu.VMEM((2, GLOB, BLOCK, keys.shape[1]), BF),
                pltpu.SemaphoreType.DMA((6,)),
                pltpu.SemaphoreType.DMA((2 * GLOB,)),
            ],
        ),
        out_shape=[jax.ShapeDtypeStruct(x, BF) for x in shapes],
        compiler_params=params(),
        cost_estimate=CHEAP,
    )(random_blocks, global_blocks, q, keys, values)


def pack(asked, sources, pieces):
    step = 8
    arrays = []
    for x, _ in sources:
        if not any(x is y for y in arrays):
            arrays.append(x)
    tiles = [([x is y for y in arrays].index(True), at * HEAD) for x, at in sources]
    widths = [max(at for m, at in tiles if m == n) + HEAD for n in range(len(arrays))]
    extra = pieces.shape[0]
    slot_rows = len(tiles) * BLOCK + extra

    def body(ask, *refs):
        p_ref, out = refs[-2:]
        base = pl.program_id(0) * step
        for d in range(step):
            rows = pl.ds(pl.multiple_of(ask[base + d] * BLOCK, BLOCK), BLOCK)
            for t, (n, at) in enumerate(tiles):
                out[d, t * BLOCK : (t + 1) * BLOCK] = refs[n][rows, at : at + HEAD]
            out[d, len(tiles) * BLOCK :] = p_ref[...]

    def whole(*shape):
        return pl.BlockSpec(shape, lambda i, *_: (0, 0))

    return pl.pallas_call(
        body,
        grid_spec=pltpu.PrefetchScalarGridSpec(
            num_scalar_prefetch=1,
            grid=(DEVS // step,),
            in_specs=[whole(ROWS, w) for w in widths] + [whole(*pieces.shape)],
            out_specs=pl.BlockSpec((step, slot_rows, HEAD), lambda i, *_: (i, 0, 0)),
        ),
        out_shape=jax.ShapeDtypeStruct((DEVS, slot_rows, HEAD), BF),
        compiler_params=params(),
        cost_estimate=CHEAP,
    )(asked, *arrays, pieces)


def pack_first(holder, keys, values, message, owners):
    step = 8
    tiles = 2 * LATE
    cut = LATE * HEAD
    kept = (LATE + 1) // 2 * PIECE
    split = LATE // 2 * PIECE
    pieces = PAIRS * PIECE
    slot_rows = tiles * BLOCK + kept

    def body(held, k_ref, v_ref, ask_ref, p_ref, own_ref, out, notes):
        base = pl.program_id(0) * step
        ask = ask_ref[pl.ds(base, step), 0:1, :].astype(jnp.float32).astype(jnp.int32)
        for d in range(step):
            rows = pl.ds(pl.multiple_of(ask[d, 0, 0] * BLOCK, BLOCK), BLOCK)
            for t in range(tiles):
                src, at = (k_ref, v_ref)[t // LATE], t % LATE * HEAD
                out[d, t * BLOCK : (t + 1) * BLOCK] = src[rows, at : at + HEAD]
            out[d, tiles * BLOCK :] = p_ref[0, :kept]

        @pl.when(pl.program_id(0) == 0)
        def _():
            notes[: pieces - split] = p_ref[0, split:]
            notes[pieces - split : pieces - split + DEVS] = ask_ref[:, 0, :]
            notes[pieces - split + DEVS :] = own_ref[...]

    notes_rows = pieces - split + DEVS + PIECE
    return pl.pallas_call(
        body,
        grid_spec=pltpu.PrefetchScalarGridSpec(
            num_scalar_prefetch=1,
            grid=(DEVS // step,),
            in_specs=[
                pl.BlockSpec((ROWS, cut), lambda i, *_: (0, 0)),
                pl.BlockSpec((ROWS, cut), lambda i, *_: (0, 0)),
                pl.BlockSpec((DEVS, PIECE, HEAD), lambda i, *_: (0, PAIRS, 0)),
                pl.BlockSpec((1, pieces, HEAD), lambda i, held: (held[0], 0, 0)),
                pl.BlockSpec((PIECE, HEAD), lambda i, *_: (0, 0)),
            ],
            out_specs=[
                pl.BlockSpec((step, slot_rows, HEAD), lambda i, *_: (i, 0, 0)),
                pl.BlockSpec((notes_rows, HEAD), lambda i, *_: (0, 0)),
            ],
        ),
        out_shape=[
            jax.ShapeDtypeStruct((DEVS, slot_rows, HEAD), BF),
            jax.ShapeDtypeStruct((notes_rows, HEAD), BF),
        ],
        compiler_params=params(),
        cost_estimate=CHEAP,
    )(holder, keys, values, message, message, owners)


def attention(slots, flags, heads, first, qs, k, k_at, v, v_at, before, after, halo_at, got, got_first, got_heads, width=None, out=None):
    hk_at, hv_at = halo_at
    cuts = 1
    half = BLOCKS // cuts
    part_rows = half * BLOCK
    counts = [n for _, _, n in qs]
    starts = [sum(counts[:i]) for i in range(len(qs))]

    def body(slot, flag, *refs):
        q_refs = refs[: len(qs)]
        k_ref, v_ref, kb, vb, ka, va, rk, rv, gl, *rest = refs[len(qs) :]
        o_ref, kpad, vpad, kcat, vcat, *q_scratch = rest[-5 - (len(qs) > 1) :] if len(qs) > 1 else rest[-5:]
        h, part = pl.program_id(0), pl.program_id(1)
        if len(qs) > 1:
            q_ref = q_scratch[0]
            for i, some in enumerate(q_refs):
                @pl.when((h >= starts[i]) & (h < starts[i] + counts[i]))
                def _(some=some):
                    q_ref[...] = some[...]
        else:
            q_ref = q_refs[0]

        @pl.when(part == 0)
        def _():
            odd = lax.rem(first + h, 2)
            for pad, own, b, a in ((kpad, k_ref, kb, ka), (vpad, v_ref, vb, va)):
                pad[0:BLOCK] = b[...]
                pad[BLOCK : BLOCK + ROWS] = own[...]
                pad[BLOCK + ROWS :] = a[...]
            for buf in range(2):
                for g in range(GLOB):
                    for i in range(4):
                        at = 3 * BLOCK + g * BLOCK + i * PIECE
                        kcat[buf, at : at + PIECE] = gl[g * 16 + odd * 4 + i]
                        vcat[buf, at : at + PIECE, 0:HEAD] = gl[g * 16 + (2 + odd) * 4 + i]
                vcat[buf, :, HEAD:] = jnp.ones((KEYS, HEAD), BF)

        for j in range(half):
            buf = j % 2
            window = pl.ds(pl.multiple_of(part * part_rows + j * BLOCK, BLOCK), 3 * BLOCK)
            kcat[buf, 0 : 3 * BLOCK] = kpad[window]
            vcat[buf, 0 : 3 * BLOCK, 0:HEAD] = vpad[window]
            for r in range(RAND):
                s = slot[(part * half + j) * RAND + r]
                at = (3 + GLOB + r) * BLOCK
                kcat[buf, at : at + BLOCK] = rk[s]
                vcat[buf, at : at + BLOCK, 0:HEAD] = rv[s]
            rows = slice(j * BLOCK, (j + 1) * BLOCK)
            part_heads = 2
            for u in range(GROUP // part_heads):
                mine = range(u * part_heads, (u + 1) * part_heads)
                qq = jnp.concatenate([q_ref[rows, g * HEAD : (g + 1) * HEAD] for g in mine], axis=0)
                s = lax.dot_general(
                    qq, kcat[buf], (((1,), (1,)), ((), ())), preferred_element_type=jnp.float32
                )
                if j == 0 or j == half - 1:
                    col = lax.broadcasted_iota(jnp.int32, (1, KEYS), 1)
                    if j == 0:
                        hide = (col < BLOCK) & (flag[0] == 0) & (part == 0)
                    else:
                        hide = (col >= 2 * BLOCK) & (col < 3 * BLOCK) & (flag[1] == 0) & (part == cuts - 1)
                    s = jnp.where(hide, -jnp.inf, s)
                top = jnp.max(s, axis=-1, keepdims=True)
                e = jnp.exp2((s - top) * SCALE).astype(BF)
                o = lax.dot_general(
                    e, vcat[buf], (((1,), (0,)), ((), ())), preferred_element_type=jnp.float32
                )
                o = (o[:, :HEAD] / o[:, HEAD:]).astype(BF)
                for n, g in enumerate(mine):
                    o_ref[rows, g * HEAD : (g + 1) * HEAD] = o[n * BLOCK : (n + 1) * BLOCK]

    def col(shape, at):
        return pl.BlockSpec(shape, lambda h, *_: (0, at + h))

    def q_spec(i):
        _, at, n = qs[i]
        lo = starts[i]

        def index(h, p, *_):
            here = (h >= lo) & (h < lo + n)
            row = jnp.where(here, p, jnp.where(h < lo, 0, cuts - 1))
            return row, at + jnp.minimum(jnp.maximum(h - lo, 0), n - 1)

        return pl.BlockSpec((part_rows, QW), index)

    at = first - got_first
    glob_at = 2 * got_heads * BLOCK // PIECE - got_first // 2
    in_specs = [q_spec(i) for i in range(len(qs))] + [
        col((ROWS, HEAD), k_at),
        col((ROWS, HEAD), v_at),
        col((BLOCK, HEAD), hk_at),
        col((BLOCK, HEAD), hv_at),
        col((BLOCK, HEAD), hk_at),
        col((BLOCK, HEAD), hv_at),
        pl.BlockSpec((DEVS, BLOCK, HEAD), lambda h, *_: (0, at + h, 0)),
        pl.BlockSpec((DEVS, BLOCK, HEAD), lambda h, *_: (0, got_heads + at + h, 0)),
        pl.BlockSpec((DEVS, PIECE, HEAD), lambda h, *_: (0, glob_at + lax.div(first + h, 2), 0)),
    ]
    operands = [slots, flags, *[x for x, _, _ in qs], k, v, before, before, after, after, got, got, got]
    aliases = {}
    if out is not None:
        in_specs.append(pl.BlockSpec(memory_space=pl.ANY))
        aliases = {len(operands): 0}
        operands.append(out)
    out_at = first if width else 0
    scratch = [
        pltpu.VMEM((ROWS + 2 * BLOCK, HEAD), BF),
        pltpu.VMEM((ROWS + 2 * BLOCK, HEAD), BF),
        pltpu.VMEM((2, KEYS, HEAD), BF),
        pltpu.VMEM((2, KEYS, 2 * HEAD), BF),
    ]
    if len(qs) > 1:
        scratch.append(pltpu.VMEM((part_rows, QW), BF))
    return pl.pallas_call(
        body,
        grid_spec=pltpu.PrefetchScalarGridSpec(
            num_scalar_prefetch=2,
            grid=(heads, cuts),
            in_specs=in_specs,
            out_specs=pl.BlockSpec((part_rows, QW), lambda h, p, *_: (p, out_at + h)),
            scratch_shapes=scratch,
        ),
        out_shape=jax.ShapeDtypeStruct((ROWS, width or heads * QW), BF),
        input_output_aliases=aliases,
        compiler_params=params(),
        cost_estimate=attention_cost(heads),
    )(*operands)


def place(part, out, at, width=None):
    step = ROWS // 2

    def body(p_ref, *refs):
        refs[-1][...] = p_ref[...]

    in_specs = [pl.BlockSpec((step, part.shape[1]), lambda i: (i, 0))]
    operands = [part]
    if out is not None:
        in_specs.append(pl.BlockSpec(memory_space=pl.ANY))
        operands.append(out)
        width = out.shape[1]
    return pl.pallas_call(
        body,
        grid=(2,),
        in_specs=in_specs,
        out_specs=pl.BlockSpec((step, part.shape[1]), lambda i: (i, at)),
        out_shape=jax.ShapeDtypeStruct((ROWS, width), BF),
        input_output_aliases={} if out is None else {1: 0},
        compiler_params=params(),
        cost_estimate=CHEAP,
    )(*operands)


def tied(x, *others):
    return lax.optimization_barrier((x, *others))[0]


def per_device(queries, keys_in, values_in, random_blocks, global_blocks):
    q, keys, values = queries[0], keys_in[0], values_in[0]
    me = lax.axis_index("seq")
    early_heads = HEADS_KV - LATE
    cut = LATE * HEAD
    near_cols = slice(LATE * QW, (HEADS_KV - FAR) * QW)
    always = me >= 0
    holder = jnp.where(me < DEVS // GLOB, global_blocks[0, :1], global_blocks[0, 1:]) // BLOCKS
    owners = random_blocks[0].reshape(BLOCKS * RAND) // BLOCKS
    flags = jnp.stack([me > 0, me < DEVS - 1]).astype(jnp.int32)

    first, high, far_a = opening(random_blocks[0].T, global_blocks[0], q, keys, values)
    high = along(high, "segment", 1)
    far_a = along(far_a, "segment", -1)

    def ask(first, q):
        return exchange(first), q[:, near_cols], q[:, (HEADS_KV - 1) * QW :]

    def no_ask(first, q):
        near = jnp.zeros((ROWS, near_cols.stop - near_cols.start), BF)
        return jnp.zeros_like(first), near, jnp.zeros((ROWS, QW), BF)

    message, near_q, far_b = lax.cond(always, ask, no_ask, first, q)
    message, far_a = lax.optimization_barrier((message, far_a))
    own_row = jnp.concatenate([owners, jnp.zeros((HEAD - BLOCKS * RAND,), jnp.int32)]).astype(BF)
    packed, notes = pack_first(
        holder, keys, values, message, jnp.broadcast_to(own_row[None], (PIECE, HEAD))
    )
    notes = along(notes, "segment", 1)
    near_q = along(tied(near_q, notes), "segment", 1)
    far_b = along(far_b, "segment", -1)
    packed, high, notes, far_a = lax.optimization_barrier((packed, high, notes, far_a))
    asked_at = notes.shape[0] - PIECE - DEVS
    asked_e = notes[asked_at:-PIECE, 0].astype(jnp.int32)
    owners_e = notes[-PIECE, : BLOCKS * RAND].astype(jnp.int32)

    def edge(rows):
        return jnp.concatenate([keys[rows, :cut], values[rows, :cut], high[rows]], axis=1)

    def middle(packed, far, asked_e, pieces_e):
        got = exchange(packed)
        far = along(far, "segment", -1)
        before = along(edge(slice(ROWS - BLOCK, ROWS)), "seq", 1)
        after = along(edge(slice(0, BLOCK)), "seq", -1)
        packed_e = pack(asked_e, [(high, c) for c in range(2 * early_heads)], pieces_e)
        return got, far, before, after, packed_e

    def no_middle(packed, far, asked_e, pieces_e):
        side = jnp.zeros((BLOCK, 2 * keys.shape[1]), BF)
        packed_e = jnp.zeros((DEVS, 2 * early_heads * BLOCK + pieces_e.shape[0], HEAD), BF)
        return jnp.zeros_like(packed), jnp.zeros_like(far), side, side, packed_e

    got, far_a, before, after, packed = lax.cond(
        always, middle, no_middle, packed, far_a, asked_e, notes[:asked_at]
    )
    got_e = exchange(packed)

    sent = []
    slots = owners
    far_a = along(far_a, "segment", -1)
    far_b = along(tied(far_b, got), "segment", -1)
    for h in range(LATE):
        if h == 1:
            slots, near_q, far_b = lax.optimization_barrier((slots, near_q, far_b))
        res = attention(
            slots, flags, 1, h, [(q, h, 1)], keys, h, values, h, before, after, (h, LATE + h), got, 0, LATE
        )
        slots = tied(owners, res)
        sent.append(along(res, "segment", 1))
    far_b = along(tied(far_b, res), "segment", -1)

    out = place(tied(sent[0], res), None, 0, q.shape[1])
    out = place(tied(sent[1], res), out, 1)
    parts = [(near_q, 0, early_heads - FAR), (far_a, 0, 1), (far_b, 0, 1)]
    out = attention(
        owners_e, flags, early_heads, LATE, parts, high, 0, high, early_heads, before, after,
        (2 * LATE, 2 * LATE + early_heads), got_e, LATE, early_heads, width=q.shape[1], out=out,
    )
    for h in range(2, LATE):
        out = place(sent[h], out, h)
    return out[None]


def solution(mesh):
    in_specs = (
        P("segment", "seq", None),
        P("segment", "seq", None),
        P("segment", "seq", None),
        P("segment", "seq", None),
        P("segment", None),
    )
    out_specs = P("segment", "seq", None)
    return jax.shard_map(
        per_device, mesh=mesh, in_specs=in_specs, out_specs=out_specs, check_vma=False
    )
```

```python
import math

import jax
import jax.numpy as jnp
from jax import lax
from jax.experimental import pallas as pl
from jax.experimental.pallas import tpu as pltpu
from jax.sharding import PartitionSpec as P

HEAD = 128
BLOCK = 64
GLOB = 2
RAND = 3
ROWS = 512
BLOCKS = ROWS // BLOCK
GROUP = 8
HEADS_KV = 8
PAIRS = HEADS_KV // 2
LATE = 3
FAR = 2
DEVS = 32
PIECE = 16
KEYS = 512
WEIGHT = 20
QW = GROUP * HEAD
BF = jnp.bfloat16
SCALE = math.log2(math.e) / math.sqrt(HEAD)
VMEM_BYTES = 63 << 20
CHEAP = pl.CostEstimate(flops=0, bytes_accessed=0, transcendentals=0)


def attention_cost(heads):
    scores = heads * GROUP * ROWS * KEYS
    return pl.CostEstimate(
        flops=WEIGHT * 4 * scores * HEAD, bytes_accessed=WEIGHT * 4 * heads * ROWS * QW, transcendentals=scores
    )


def along(x, axis, by):
    n = lax.axis_size(axis)
    return lax.ppermute(x, axis, [(i, (i + by) % n) for i in range(n)])


def exchange(x):
    return lax.all_to_all(x, "seq", split_axis=0, concat_axis=0, tiled=True)


def params():
    return pltpu.CompilerParams(vmem_limit_bytes=VMEM_BYTES)


def opening(random_blocks, global_blocks, q, keys, values):
    cut = LATE * HEAD
    rest = keys.shape[1] - cut
    message_shape = (DEVS, (PAIRS + 1) * PIECE, HEAD)
    shapes = [message_shape, (ROWS, 2 * rest), (ROWS, QW)]

    def body(rb, gb, q_ref, k_ref, v_ref, out_hbm, high_hbm, far_hbm, out, high, far, glob, sems, glob_sems):
        base = lax.axis_index("seq") * BLOCKS
        globs = []
        for g in range(GLOB):
            at = jnp.minimum(jnp.maximum(gb[g] - base, 0), BLOCKS - 1) * BLOCK
            rows = pl.ds(pl.multiple_of(at, BLOCK), BLOCK)
            for n, src in enumerate((k_ref, v_ref)):
                globs.append(pltpu.make_async_copy(src.at[rows], glob.at[n, g], glob_sems.at[2 * n + g]))
        loads = [
            pltpu.make_async_copy(k_ref.at[:, pl.ds(cut, rest)], high.at[:, pl.ds(0, rest)], sems.at[0]),
            pltpu.make_async_copy(v_ref.at[:, pl.ds(cut, rest)], high.at[:, pl.ds(rest, rest)], sems.at[1]),
            pltpu.make_async_copy(q_ref.at[:, pl.ds((HEADS_KV - FAR) * QW, QW)], far, sems.at[2]),
        ]
        stores = [
            pltpu.make_async_copy(high, high_hbm, sems.at[3]),
            pltpu.make_async_copy(far, far_hbm, sems.at[4]),
            pltpu.make_async_copy(out, out_hbm, sems.at[5]),
        ]
        for c in loads + globs:
            c.start()
        out[:, PAIRS * PIECE :] = jnp.zeros((DEVS, PIECE, HEAD), BF)
        for r in range(RAND):
            for j in range(BLOCKS):
                wanted = rb[r, j]
                out[lax.shift_right_logical(wanted, 3), PAIRS * PIECE :] = jnp.full(
                    (PIECE, HEAD), wanted & (BLOCKS - 1), jnp.int32
                ).astype(jnp.float32).astype(BF)
        loads[0].wait()
        loads[1].wait()
        stores[0].start()
        loads[2].wait()
        stores[1].start()
        for c in globs:
            c.wait()
        for i in range(DEVS):
            g, t, part = i // 16, (i % 16) // 4, i % 4
            for c in range(PAIRS):
                head = 2 * c + t % 2
                out[i, c * PIECE : (c + 1) * PIECE] = glob[
                    t // 2, g, part * PIECE : (part + 1) * PIECE, head * HEAD : (head + 1) * HEAD
                ]
        stores[2].start()
        for c in stores:
            c.wait()

    here = pl.BlockSpec(memory_space=pltpu.HBM)
    return pl.pallas_call(
        body,
        grid_spec=pltpu.PrefetchScalarGridSpec(
            num_scalar_prefetch=2,
            grid=(1,),
            in_specs=[here] * 3,
            out_specs=[here] * 3,
            scratch_shapes=[pltpu.VMEM(x, BF) for x in shapes]
            + [
                pltpu.VMEM((2, GLOB, BLOCK, keys.shape[1]), BF),
                pltpu.SemaphoreType.DMA((6,)),
                pltpu.SemaphoreType.DMA((2 * GLOB,)),
            ],
        ),
        out_shape=[jax.ShapeDtypeStruct(x, BF) for x in shapes],
        compiler_params=params(),
        cost_estimate=CHEAP,
    )(random_blocks, global_blocks, q, keys, values)


def pack(asked, sources, pieces):
    step = 8
    arrays = []
    for x, _ in sources:
        if not any(x is y for y in arrays):
            arrays.append(x)
    tiles = [([x is y for y in arrays].index(True), at * HEAD) for x, at in sources]
    widths = [max(at for m, at in tiles if m == n) + HEAD for n in range(len(arrays))]
    extra = pieces.shape[0]
    slot_rows = len(tiles) * BLOCK + extra

    def body(ask, *refs):
        p_ref, out = refs[-2:]
        base = pl.program_id(0) * step
        for d in range(step):
            rows = pl.ds(pl.multiple_of(ask[base + d] * BLOCK, BLOCK), BLOCK)
            for t, (n, at) in enumerate(tiles):
                out[d, t * BLOCK : (t + 1) * BLOCK] = refs[n][rows, at : at + HEAD]
            out[d, len(tiles) * BLOCK :] = p_ref[...]

    def whole(*shape):
        return pl.BlockSpec(shape, lambda i, *_: (0, 0))

    return pl.pallas_call(
        body,
        grid_spec=pltpu.PrefetchScalarGridSpec(
            num_scalar_prefetch=1,
            grid=(DEVS // step,),
            in_specs=[whole(ROWS, w) for w in widths] + [whole(*pieces.shape)],
            out_specs=pl.BlockSpec((step, slot_rows, HEAD), lambda i, *_: (i, 0, 0)),
        ),
        out_shape=jax.ShapeDtypeStruct((DEVS, slot_rows, HEAD), BF),
        compiler_params=params(),
        cost_estimate=CHEAP,
    )(asked, *arrays, pieces)


def pack_first(holder, keys, values, message, owners):
    step = 8
    tiles = 2 * LATE
    cut = LATE * HEAD
    kept = (LATE + 1) // 2 * PIECE
    split = LATE // 2 * PIECE
    pieces = PAIRS * PIECE
    slot_rows = tiles * BLOCK + kept

    def body(held, k_ref, v_ref, ask_ref, p_ref, own_ref, out, notes):
        base = pl.program_id(0) * step
        ask = ask_ref[pl.ds(base, step), 0:1, :].astype(jnp.float32).astype(jnp.int32)
        for d in range(step):
            rows = pl.ds(pl.multiple_of(ask[d, 0, 0] * BLOCK, BLOCK), BLOCK)
            for t in range(tiles):
                src, at = (k_ref, v_ref)[t // LATE], t % LATE * HEAD
                out[d, t * BLOCK : (t + 1) * BLOCK] = src[rows, at : at + HEAD]
            out[d, tiles * BLOCK :] = p_ref[0, :kept]

        @pl.when(pl.program_id(0) == 0)
        def _():
            notes[: pieces - split] = p_ref[0, split:]
            notes[pieces - split : pieces - split + DEVS] = ask_ref[:, 0, :]
            notes[pieces - split + DEVS :] = own_ref[...]

    notes_rows = pieces - split + DEVS + PIECE
    return pl.pallas_call(
        body,
        grid_spec=pltpu.PrefetchScalarGridSpec(
            num_scalar_prefetch=1,
            grid=(DEVS // step,),
            in_specs=[
                pl.BlockSpec((ROWS, cut), lambda i, *_: (0, 0)),
                pl.BlockSpec((ROWS, cut), lambda i, *_: (0, 0)),
                pl.BlockSpec((DEVS, PIECE, HEAD), lambda i, *_: (0, PAIRS, 0)),
                pl.BlockSpec((1, pieces, HEAD), lambda i, held: (held[0], 0, 0)),
                pl.BlockSpec((PIECE, HEAD), lambda i, *_: (0, 0)),
            ],
            out_specs=[
                pl.BlockSpec((step, slot_rows, HEAD), lambda i, *_: (i, 0, 0)),
                pl.BlockSpec((notes_rows, HEAD), lambda i, *_: (0, 0)),
            ],
        ),
        out_shape=[
            jax.ShapeDtypeStruct((DEVS, slot_rows, HEAD), BF),
            jax.ShapeDtypeStruct((notes_rows, HEAD), BF),
        ],
        compiler_params=params(),
        cost_estimate=CHEAP,
    )(holder, keys, values, message, message, owners)


def attention(slots, flags, heads, first, qs, k, k_at, v, v_at, before, after, halo_at, got, got_first, got_heads, width=None, out=None):
    hk_at, hv_at = halo_at
    cuts = 1
    half = BLOCKS // cuts
    part_rows = half * BLOCK
    counts = [n for _, _, n in qs]
    starts = [sum(counts[:i]) for i in range(len(qs))]

    def body(slot, flag, *refs):
        q_refs = refs[: len(qs)]
        k_ref, v_ref, kb, vb, ka, va, rk, rv, gl, *rest = refs[len(qs) :]
        o_ref, kpad, vpad, kcat, vcat, *q_scratch = rest[-5 - (len(qs) > 1) :] if len(qs) > 1 else rest[-5:]
        h, part = pl.program_id(0), pl.program_id(1)
        if len(qs) > 1:
            q_ref = q_scratch[0]
            for i, some in enumerate(q_refs):
                @pl.when((h >= starts[i]) & (h < starts[i] + counts[i]))
                def _(some=some):
                    q_ref[...] = some[...]
        else:
            q_ref = q_refs[0]

        @pl.when(part == 0)
        def _():
            odd = lax.rem(first + h, 2)
            for pad, own, b, a in ((kpad, k_ref, kb, ka), (vpad, v_ref, vb, va)):
                pad[0:BLOCK] = b[...]
                pad[BLOCK : BLOCK + ROWS] = own[...]
                pad[BLOCK + ROWS :] = a[...]
            for buf in range(2):
                for g in range(GLOB):
                    for i in range(4):
                        at = 3 * BLOCK + g * BLOCK + i * PIECE
                        kcat[buf, at : at + PIECE] = gl[g * 16 + odd * 4 + i]
                        vcat[buf, at : at + PIECE, 0:HEAD] = gl[g * 16 + (2 + odd) * 4 + i]
                vcat[buf, :, HEAD:] = jnp.ones((KEYS, HEAD), BF)

        for j in range(half):
            buf = j % 2
            window = pl.ds(pl.multiple_of(part * part_rows + j * BLOCK, BLOCK), 3 * BLOCK)
            kcat[buf, 0 : 3 * BLOCK] = kpad[window]
            vcat[buf, 0 : 3 * BLOCK, 0:HEAD] = vpad[window]
            for r in range(RAND):
                s = slot[(part * half + j) * RAND + r]
                at = (3 + GLOB + r) * BLOCK
                kcat[buf, at : at + BLOCK] = rk[s]
                vcat[buf, at : at + BLOCK, 0:HEAD] = rv[s]
            rows = slice(j * BLOCK, (j + 1) * BLOCK)
            part_heads = 2
            for u in range(GROUP // part_heads):
                mine = range(u * part_heads, (u + 1) * part_heads)
                qq = jnp.concatenate([q_ref[rows, g * HEAD : (g + 1) * HEAD] for g in mine], axis=0)
                s = lax.dot_general(
                    qq, kcat[buf], (((1,), (1,)), ((), ())), preferred_element_type=jnp.float32
                )
                if j == 0 or j == half - 1:
                    col = lax.broadcasted_iota(jnp.int32, (1, KEYS), 1)
                    if j == 0:
                        hide = (col < BLOCK) & (flag[0] == 0) & (part == 0)
                    else:
                        hide = (col >= 2 * BLOCK) & (col < 3 * BLOCK) & (flag[1] == 0) & (part == cuts - 1)
                    s = jnp.where(hide, -jnp.inf, s)
                top = jnp.max(s, axis=-1, keepdims=True)
                e = jnp.exp2((s - top) * SCALE).astype(BF)
                o = lax.dot_general(
                    e, vcat[buf], (((1,), (0,)), ((), ())), preferred_element_type=jnp.float32
                )
                o = (o[:, :HEAD] / o[:, HEAD:]).astype(BF)
                for n, g in enumerate(mine):
                    o_ref[rows, g * HEAD : (g + 1) * HEAD] = o[n * BLOCK : (n + 1) * BLOCK]

    def col(shape, at):
        return pl.BlockSpec(shape, lambda h, *_: (0, at + h))

    def q_spec(i):
        _, at, n = qs[i]
        lo = starts[i]

        def index(h, p, *_):
            here = (h >= lo) & (h < lo + n)
            row = jnp.where(here, p, jnp.where(h < lo, 0, cuts - 1))
            return row, at + jnp.minimum(jnp.maximum(h - lo, 0), n - 1)

        return pl.BlockSpec((part_rows, QW), index)

    at = first - got_first
    glob_at = 2 * got_heads * BLOCK // PIECE - got_first // 2
    in_specs = [q_spec(i) for i in range(len(qs))] + [
        col((ROWS, HEAD), k_at),
        col((ROWS, HEAD), v_at),
        col((BLOCK, HEAD), hk_at),
        col((BLOCK, HEAD), hv_at),
        col((BLOCK, HEAD), hk_at),
        col((BLOCK, HEAD), hv_at),
        pl.BlockSpec((DEVS, BLOCK, HEAD), lambda h, *_: (0, at + h, 0)),
        pl.BlockSpec((DEVS, BLOCK, HEAD), lambda h, *_: (0, got_heads + at + h, 0)),
        pl.BlockSpec((DEVS, PIECE, HEAD), lambda h, *_: (0, glob_at + lax.div(first + h, 2), 0)),
    ]
    operands = [slots, flags, *[x for x, _, _ in qs], k, v, before, before, after, after, got, got, got]
    aliases = {}
    if out is not None:
        in_specs.append(pl.BlockSpec(memory_space=pl.ANY))
        aliases = {len(operands): 0}
        operands.append(out)
    out_at = first if width else 0
    scratch = [
        pltpu.VMEM((ROWS + 2 * BLOCK, HEAD), BF),
        pltpu.VMEM((ROWS + 2 * BLOCK, HEAD), BF),
        pltpu.VMEM((2, KEYS, HEAD), BF),
        pltpu.VMEM((2, KEYS, 2 * HEAD), BF),
    ]
    if len(qs) > 1:
        scratch.append(pltpu.VMEM((part_rows, QW), BF))
    return pl.pallas_call(
        body,
        grid_spec=pltpu.PrefetchScalarGridSpec(
            num_scalar_prefetch=2,
            grid=(heads, cuts),
            in_specs=in_specs,
            out_specs=pl.BlockSpec((part_rows, QW), lambda h, p, *_: (p, out_at + h)),
            scratch_shapes=scratch,
        ),
        out_shape=jax.ShapeDtypeStruct((ROWS, width or heads * QW), BF),
        input_output_aliases=aliases,
        compiler_params=params(),
        cost_estimate=attention_cost(heads),
    )(*operands)


def place(part, out, at, width=None):
    step = ROWS // 2

    def body(p_ref, *refs):
        refs[-1][...] = p_ref[...]

    in_specs = [pl.BlockSpec((step, part.shape[1]), lambda i: (i, 0))]
    operands = [part]
    if out is not None:
        in_specs.append(pl.BlockSpec(memory_space=pl.ANY))
        operands.append(out)
        width = out.shape[1]
    return pl.pallas_call(
        body,
        grid=(2,),
        in_specs=in_specs,
        out_specs=pl.BlockSpec((step, part.shape[1]), lambda i: (i, at)),
        out_shape=jax.ShapeDtypeStruct((ROWS, width), BF),
        input_output_aliases={} if out is None else {1: 0},
        compiler_params=params(),
        cost_estimate=CHEAP,
    )(*operands)


def tied(x, *others):
    return lax.optimization_barrier((x, *others))[0]


def per_device(queries, keys_in, values_in, random_blocks, global_blocks):
    q, keys, values = queries[0], keys_in[0], values_in[0]
    me = lax.axis_index("seq")
    early_heads = HEADS_KV - LATE
    cut = LATE * HEAD
    near_cols = slice(LATE * QW, (HEADS_KV - FAR) * QW)
    always = me >= 0

    first, high, far_a = opening(random_blocks[0].T, global_blocks[0], q, keys, values)
    high = along(high, "segment", 1)
    far_a = along(far_a, "segment", -1)

    def edges(*parts):
        last = jnp.concatenate([x[ROWS - BLOCK :] for x in parts], axis=1)
        leading = jnp.concatenate([x[:BLOCK] for x in parts], axis=1)
        return along(last, "seq", 1), along(leading, "seq", -1)

    def ask(first, q, blocks, listed):
        owners = blocks.reshape(BLOCKS * RAND) // BLOCKS
        row = jnp.concatenate([owners, jnp.zeros((HEAD - BLOCKS * RAND,), jnp.int32)]).astype(BF)
        holder = jnp.where(me < DEVS // GLOB, listed[:1], listed[1:]) // BLOCKS
        flags = jnp.stack([me > 0, me < DEVS - 1]).astype(jnp.int32)
        return (
            exchange(first), q[:, near_cols], q[:, (HEADS_KV - 1) * QW :],
            owners, jnp.broadcast_to(row[None], (PIECE, HEAD)), holder, flags, *edges(keys[:, :cut], values[:, :cut]),
        )

    def ask_shapes(q):
        ints = [jnp.zeros((n,), jnp.int32) for n in (BLOCKS * RAND, 1, 2)]
        return (
            jnp.zeros(first.shape, BF), q[:, near_cols], q[:, :QW],
            ints[0], jnp.zeros((PIECE, HEAD), BF), ints[1], ints[2],
            jnp.zeros((BLOCK, 2 * cut), BF), jnp.zeros((BLOCK, 2 * cut), BF),
        )

    def no_ask(first, q, blocks, listed):
        return jax.tree.map(lambda x: jnp.zeros(x.shape, x.dtype), jax.eval_shape(ask_shapes, q))

    message, near_q, far_b, owners, own_tile, holder, flags, before, after = lax.cond(
        always, ask, no_ask, first, q, random_blocks[0], global_blocks[0]
    )
    packed, notes = pack_first(holder, keys, values, message, own_tile)
    notes = along(notes, "segment", 1)
    packed, notes, far_a, high = lax.optimization_barrier((packed, notes, far_a, high))
    got = exchange(packed)
    near_q = along(tied(near_q, notes), "segment", 1)
    far_b = along(tied(far_b, notes), "segment", -1)
    far_a = along(tied(far_a, notes), "segment", -1)
    asked_at = notes.shape[0] - PIECE - DEVS
    asked_e = notes[asked_at:-PIECE, 0].astype(jnp.int32)
    owners_e = notes[-PIECE, : BLOCKS * RAND].astype(jnp.int32)

    before_e, after_e = edges(high)
    packed = pack(asked_e, [(high, c) for c in range(2 * early_heads)], notes[:asked_at])
    got_e = exchange(packed)

    sent = []
    slots = owners
    far_a = along(tied(far_a, got), "segment", -1)
    far_b = along(tied(far_b, got), "segment", -1)
    for h in range(LATE):
        if h == 1:
            slots, near_q, far_b = lax.optimization_barrier((slots, near_q, far_b))
        res = attention(
            slots, flags, 1, h, [(q, h, 1)], keys, h, values, h, before, after, (h, LATE + h), got, 0, LATE
        )
        slots = tied(owners, res)
        sent.append(along(res, "segment", 1))
    far_b = along(tied(far_b, res), "segment", -1)

    out = place(tied(sent[0], res), None, 0, q.shape[1])
    parts = [(near_q, 0, early_heads - FAR), (far_a, 0, 1), (far_b, 0, 1)]
    out = attention(
        owners_e, flags, early_heads, LATE, parts, high, 0, high, early_heads, before_e, after_e,
        (0, early_heads), got_e, LATE, early_heads, width=q.shape[1], out=out,
    )
    for h in reversed(range(1, LATE)):
        out = place(sent[h], out, h)
    return out[None]


def solution(mesh):
    in_specs = (
        P("segment", "seq", None),
        P("segment", "seq", None),
        P("segment", "seq", None),
        P("segment", "seq", None),
        P("segment", None),
    )
    out_specs = P("segment", "seq", None)
    return jax.shard_map(
        per_device, mesh=mesh, in_specs=in_specs, out_specs=out_specs, check_vma=False
    )
```

```python
import math

import jax
import jax.numpy as jnp
from jax import lax
from jax.experimental import pallas as pl
from jax.experimental.pallas import tpu as pltpu
from jax.sharding import PartitionSpec as P

HEAD = 128
BLOCK = 64
GLOB = 2
RAND = 3
ROWS = 512
BLOCKS = ROWS // BLOCK
GROUP = 8
HEADS_KV = 8
PAIRS = HEADS_KV // 2
LATE = 3
FAR = 2
DEVS = 32
PIECE = 16
KEYS = 512
WEIGHT = 20
QW = GROUP * HEAD
BF = jnp.bfloat16
SCALE = math.log2(math.e) / math.sqrt(HEAD)
VMEM_BYTES = 63 << 20
CHEAP = pl.CostEstimate(flops=0, bytes_accessed=0, transcendentals=0)


def attention_cost(heads):
    scores = heads * GROUP * ROWS * KEYS
    return pl.CostEstimate(
        flops=WEIGHT * 4 * scores * HEAD, bytes_accessed=WEIGHT * 4 * heads * ROWS * QW, transcendentals=scores
    )


def along(x, axis, by):
    n = lax.axis_size(axis)
    return lax.ppermute(x, axis, [(i, (i + by) % n) for i in range(n)])


def exchange(x):
    return lax.all_to_all(x, "seq", split_axis=0, concat_axis=0, tiled=True)


def params():
    return pltpu.CompilerParams(vmem_limit_bytes=VMEM_BYTES)


def opening(random_blocks, global_blocks, q, keys, values):
    cut = LATE * HEAD
    rest = keys.shape[1] - cut
    message_shape = (DEVS, (PAIRS + 1) * PIECE, HEAD)
    shapes = [message_shape, (ROWS, 2 * rest), (ROWS, QW)]

    def body(rb, gb, q_ref, k_ref, v_ref, out_hbm, high_hbm, far_hbm, out, high, far, glob, sems, glob_sems):
        base = lax.axis_index("seq") * BLOCKS
        globs = []
        for g in range(GLOB):
            at = jnp.minimum(jnp.maximum(gb[g] - base, 0), BLOCKS - 1) * BLOCK
            rows = pl.ds(pl.multiple_of(at, BLOCK), BLOCK)
            for n, src in enumerate((k_ref, v_ref)):
                globs.append(pltpu.make_async_copy(src.at[rows], glob.at[n, g], glob_sems.at[2 * n + g]))
        half = [pl.ds(i * ROWS // 2, ROWS // 2) for i in range(2)]
        high_loads, far_loads, high_stores, far_stores = [], [], [], []
        for i, rows in enumerate(half):
            high_loads += [
                pltpu.make_async_copy(
                    k_ref.at[rows, pl.ds(cut, rest)], high.at[rows, pl.ds(0, rest)], sems.at[i]
                ),
                pltpu.make_async_copy(
                    v_ref.at[rows, pl.ds(cut, rest)], high.at[rows, pl.ds(rest, rest)], sems.at[2 + i]
                ),
            ]
            far_loads.append(
                pltpu.make_async_copy(
                    q_ref.at[rows, pl.ds((HEADS_KV - FAR) * QW, QW)], far.at[rows], sems.at[4 + i]
                )
            )
            high_stores.append(pltpu.make_async_copy(high.at[rows], high_hbm.at[rows], sems.at[6 + i]))
            far_stores.append(pltpu.make_async_copy(far.at[rows], far_hbm.at[rows], sems.at[8 + i]))
        last_store = pltpu.make_async_copy(out, out_hbm, sems.at[10])
        for c in high_loads + far_loads + globs:
            c.start()
        out[:, PAIRS * PIECE :] = jnp.zeros((DEVS, PIECE, HEAD), BF)
        for r in range(RAND):
            for j in range(BLOCKS):
                wanted = rb[r, 0, j]
                out[lax.shift_right_logical(wanted, 3), PAIRS * PIECE :] = jnp.full(
                    (PIECE, HEAD), wanted & (BLOCKS - 1), jnp.int32
                ).astype(jnp.float32).astype(BF)
        for i in range(2):
            high_loads[2 * i].wait()
            high_loads[2 * i + 1].wait()
            high_stores[i].start()
        for i in range(2):
            far_loads[i].wait()
            far_stores[i].start()
        for c in globs:
            c.wait()
        for i in range(DEVS):
            g, t, part = i // 16, (i % 16) // 4, i % 4
            for c in range(PAIRS):
                head = 2 * c + t % 2
                out[i, c * PIECE : (c + 1) * PIECE] = glob[
                    t // 2, g, part * PIECE : (part + 1) * PIECE, head * HEAD : (head + 1) * HEAD
                ]
        last_store.start()
        for c in high_stores + far_stores + [last_store]:
            c.wait()

    here = pl.BlockSpec(memory_space=pltpu.HBM)
    return pl.pallas_call(
        body,
        grid_spec=pltpu.PrefetchScalarGridSpec(
            num_scalar_prefetch=2,
            grid=(1,),
            in_specs=[here] * 3,
            out_specs=[here] * 3,
            scratch_shapes=[pltpu.VMEM(x, BF) for x in shapes]
            + [
                pltpu.VMEM((2, GLOB, BLOCK, keys.shape[1]), BF),
                pltpu.SemaphoreType.DMA((11,)),
                pltpu.SemaphoreType.DMA((2 * GLOB,)),
            ],
        ),
        out_shape=[jax.ShapeDtypeStruct(x, BF) for x in shapes],
        compiler_params=params(),
        cost_estimate=CHEAP,
    )(random_blocks, global_blocks, q, keys, values)


def pack(asked, sources, pieces):
    step = 8
    arrays = []
    for x, _ in sources:
        if not any(x is y for y in arrays):
            arrays.append(x)
    tiles = [([x is y for y in arrays].index(True), at * HEAD) for x, at in sources]
    widths = [max(at for m, at in tiles if m == n) + HEAD for n in range(len(arrays))]
    extra = pieces.shape[0]
    slot_rows = len(tiles) * BLOCK + extra

    def body(ask, *refs):
        p_ref, out = refs[-2:]
        base = pl.program_id(0) * step
        for d in range(step):
            rows = pl.ds(pl.multiple_of(ask[base + d] * BLOCK, BLOCK), BLOCK)
            for t, (n, at) in enumerate(tiles):
                out[d, t * BLOCK : (t + 1) * BLOCK] = refs[n][rows, at : at + HEAD]
            out[d, len(tiles) * BLOCK :] = p_ref[...]

    def whole(*shape):
        return pl.BlockSpec(shape, lambda i, *_: (0, 0))

    return pl.pallas_call(
        body,
        grid_spec=pltpu.PrefetchScalarGridSpec(
            num_scalar_prefetch=1,
            grid=(DEVS // step,),
            in_specs=[whole(ROWS, w) for w in widths] + [whole(*pieces.shape)],
            out_specs=pl.BlockSpec((step, slot_rows, HEAD), lambda i, *_: (i, 0, 0)),
        ),
        out_shape=jax.ShapeDtypeStruct((DEVS, slot_rows, HEAD), BF),
        compiler_params=params(),
        cost_estimate=CHEAP,
    )(asked, *arrays, pieces)


def pack_first(holder, keys, values, message, owners):
    step = 8
    tiles = 2 * LATE
    cut = LATE * HEAD
    kept = (LATE + 1) // 2 * PIECE
    split = LATE // 2 * PIECE
    pieces = PAIRS * PIECE
    slot_rows = tiles * BLOCK + kept

    def body(held, k_ref, v_ref, ask_ref, p_ref, own_ref, out, notes):
        base = pl.program_id(0) * step
        ask = ask_ref[pl.ds(base, step), 0:1, :].astype(jnp.float32).astype(jnp.int32)
        for d in range(step):
            rows = pl.ds(pl.multiple_of(ask[d, 0, 0] * BLOCK, BLOCK), BLOCK)
            for t in range(tiles):
                src, at = (k_ref, v_ref)[t // LATE], t % LATE * HEAD
                out[d, t * BLOCK : (t + 1) * BLOCK] = src[rows, at : at + HEAD]
            out[d, tiles * BLOCK :] = p_ref[0, :kept]

        @pl.when(pl.program_id(0) == 0)
        def _():
            notes[: pieces - split] = p_ref[0, split:]
            notes[pieces - split : pieces - split + DEVS] = ask_ref[:, 0, :]
            notes[pieces - split + DEVS :] = own_ref[...]

    notes_rows = pieces - split + DEVS + PIECE
    return pl.pallas_call(
        body,
        grid_spec=pltpu.PrefetchScalarGridSpec(
            num_scalar_prefetch=1,
            grid=(DEVS // step,),
            in_specs=[
                pl.BlockSpec((ROWS, cut), lambda i, *_: (0, 0)),
                pl.BlockSpec((ROWS, cut), lambda i, *_: (0, 0)),
                pl.BlockSpec((DEVS, PIECE, HEAD), lambda i, *_: (0, PAIRS, 0)),
                pl.BlockSpec((1, pieces, HEAD), lambda i, held: (held[0], 0, 0)),
                pl.BlockSpec((PIECE, HEAD), lambda i, *_: (0, 0)),
            ],
            out_specs=[
                pl.BlockSpec((step, slot_rows, HEAD), lambda i, *_: (i, 0, 0)),
                pl.BlockSpec((notes_rows, HEAD), lambda i, *_: (0, 0)),
            ],
        ),
        out_shape=[
            jax.ShapeDtypeStruct((DEVS, slot_rows, HEAD), BF),
            jax.ShapeDtypeStruct((notes_rows, HEAD), BF),
        ],
        compiler_params=params(),
        cost_estimate=CHEAP,
    )(holder, keys, values, message, message, owners)


def attention(slots, flags, heads, first, qs, k, k_at, v, v_at, before, after, halo_at, got, got_first, got_heads, width=None, out=None):
    hk_at, hv_at = halo_at
    cuts = 1
    half = BLOCKS // cuts
    part_rows = half * BLOCK
    counts = [n for _, _, n in qs]
    starts = [sum(counts[:i]) for i in range(len(qs))]

    def body(slot, flag, *refs):
        q_refs = refs[: len(qs)]
        k_ref, v_ref, kb, vb, ka, va, rk, rv, gl, *rest = refs[len(qs) :]
        o_ref, kpad, vpad, kcat, vcat, *q_scratch = rest[-5 - (len(qs) > 1) :] if len(qs) > 1 else rest[-5:]
        h, part = pl.program_id(0), pl.program_id(1)
        if len(qs) > 1:
            q_ref = q_scratch[0]
            for i, some in enumerate(q_refs):
                @pl.when((h >= starts[i]) & (h < starts[i] + counts[i]))
                def _(some=some):
                    q_ref[...] = some[...]
        else:
            q_ref = q_refs[0]

        @pl.when(part == 0)
        def _():
            odd = lax.rem(first + h, 2)
            for pad, own, b, a in ((kpad, k_ref, kb, ka), (vpad, v_ref, vb, va)):
                pad[0:BLOCK] = b[...]
                pad[BLOCK : BLOCK + ROWS] = own[...]
                pad[BLOCK + ROWS :] = a[...]
            for buf in range(2):
                for g in range(GLOB):
                    for i in range(4):
                        at = 3 * BLOCK + g * BLOCK + i * PIECE
                        kcat[buf, at : at + PIECE] = gl[g * 16 + odd * 4 + i]
                        vcat[buf, at : at + PIECE, 0:HEAD] = gl[g * 16 + (2 + odd) * 4 + i]
                vcat[buf, :, HEAD:] = jnp.ones((KEYS, HEAD), BF)

        for j in range(half):
            buf = j % 2
            window = pl.ds(pl.multiple_of(part * part_rows + j * BLOCK, BLOCK), 3 * BLOCK)
            kcat[buf, 0 : 3 * BLOCK] = kpad[window]
            vcat[buf, 0 : 3 * BLOCK, 0:HEAD] = vpad[window]
            for r in range(RAND):
                s = slot[(part * half + j) * RAND + r]
                at = (3 + GLOB + r) * BLOCK
                kcat[buf, at : at + BLOCK] = rk[s]
                vcat[buf, at : at + BLOCK, 0:HEAD] = rv[s]
            rows = slice(j * BLOCK, (j + 1) * BLOCK)
            part_heads = 2
            for u in range(GROUP // part_heads):
                mine = range(u * part_heads, (u + 1) * part_heads)
                qq = jnp.concatenate([q_ref[rows, g * HEAD : (g + 1) * HEAD] for g in mine], axis=0)
                s = lax.dot_general(
                    qq, kcat[buf], (((1,), (1,)), ((), ())), preferred_element_type=jnp.float32
                )
                if j == 0 or j == half - 1:
                    col = lax.broadcasted_iota(jnp.int32, (1, KEYS), 1)
                    if j == 0:
                        hide = (col < BLOCK) & (flag[0] == 0) & (part == 0)
                    else:
                        hide = (col >= 2 * BLOCK) & (col < 3 * BLOCK) & (flag[1] == 0) & (part == cuts - 1)
                    s = jnp.where(hide, -jnp.inf, s)
                top = jnp.max(s, axis=-1, keepdims=True)
                e = jnp.exp2((s - top) * SCALE).astype(BF)
                o = lax.dot_general(
                    e, vcat[buf], (((1,), (0,)), ((), ())), preferred_element_type=jnp.float32
                )
                o = (o[:, :HEAD] / o[:, HEAD:]).astype(BF)
                for n, g in enumerate(mine):
                    o_ref[rows, g * HEAD : (g + 1) * HEAD] = o[n * BLOCK : (n + 1) * BLOCK]

    def col(shape, at):
        return pl.BlockSpec(shape, lambda h, *_: (0, at + h))

    def q_spec(i):
        _, at, n = qs[i]
        lo = starts[i]

        def index(h, p, *_):
            here = (h >= lo) & (h < lo + n)
            row = jnp.where(here, p, jnp.where(h < lo, 0, cuts - 1))
            return row, at + jnp.minimum(jnp.maximum(h - lo, 0), n - 1)

        return pl.BlockSpec((part_rows, QW), index)

    at = first - got_first
    glob_at = 2 * got_heads * BLOCK // PIECE - got_first // 2
    in_specs = [q_spec(i) for i in range(len(qs))] + [
        col((ROWS, HEAD), k_at),
        col((ROWS, HEAD), v_at),
        col((BLOCK, HEAD), hk_at),
        col((BLOCK, HEAD), hv_at),
        col((BLOCK, HEAD), hk_at),
        col((BLOCK, HEAD), hv_at),
        pl.BlockSpec((DEVS, BLOCK, HEAD), lambda h, *_: (0, at + h, 0)),
        pl.BlockSpec((DEVS, BLOCK, HEAD), lambda h, *_: (0, got_heads + at + h, 0)),
        pl.BlockSpec((DEVS, PIECE, HEAD), lambda h, *_: (0, glob_at + lax.div(first + h, 2), 0)),
    ]
    operands = [slots, flags, *[x for x, _, _ in qs], k, v, before, before, after, after, got, got, got]
    aliases = {}
    if out is not None:
        in_specs.append(pl.BlockSpec(memory_space=pl.ANY))
        aliases = {len(operands): 0}
        operands.append(out)
    out_at = first if width else 0
    scratch = [
        pltpu.VMEM((ROWS + 2 * BLOCK, HEAD), BF),
        pltpu.VMEM((ROWS + 2 * BLOCK, HEAD), BF),
        pltpu.VMEM((2, KEYS, HEAD), BF),
        pltpu.VMEM((2, KEYS, 2 * HEAD), BF),
    ]
    if len(qs) > 1:
        scratch.append(pltpu.VMEM((part_rows, QW), BF))
    return pl.pallas_call(
        body,
        grid_spec=pltpu.PrefetchScalarGridSpec(
            num_scalar_prefetch=2,
            grid=(heads, cuts),
            in_specs=in_specs,
            out_specs=pl.BlockSpec((part_rows, QW), lambda h, p, *_: (p, out_at + h)),
            scratch_shapes=scratch,
        ),
        out_shape=jax.ShapeDtypeStruct((ROWS, width or heads * QW), BF),
        input_output_aliases=aliases,
        compiler_params=params(),
        cost_estimate=attention_cost(heads),
    )(*operands)


def place(part, out, at, width=None):
    cuts = 8
    step = ROWS // cuts

    def body(p_ref, *refs):
        o_ref, stage, load_sems, store_sems = refs[-4:]
        loads, stores = [], []
        for i in range(cuts):
            rows = pl.ds(i * step, step)
            loads.append(pltpu.make_async_copy(p_ref.at[rows], stage.at[rows], load_sems.at[i]))
            stores.append(
                pltpu.make_async_copy(stage.at[rows], o_ref.at[rows, pl.ds(at * QW, QW)], store_sems.at[i])
            )
        for c in loads:
            c.start()
        for x, y in zip(loads, stores):
            x.wait()
            y.start()
        for c in stores:
            c.wait()

    here = pl.BlockSpec(memory_space=pltpu.HBM)
    operands = [part]
    if out is not None:
        operands.append(out)
        width = out.shape[1]
    return pl.pallas_call(
        body,
        in_specs=[here] * len(operands),
        out_specs=here,
        out_shape=jax.ShapeDtypeStruct((ROWS, width), BF),
        scratch_shapes=[
            pltpu.VMEM((ROWS, QW), BF),
            pltpu.SemaphoreType.DMA((cuts,)),
            pltpu.SemaphoreType.DMA((cuts,)),
        ],
        input_output_aliases={} if out is None else {1: 0},
        compiler_params=params(),
        cost_estimate=CHEAP,
    )(*operands)


def tied(x, *others):
    return lax.optimization_barrier((x, *others))[0]


def per_device(queries, keys_in, values_in, random_blocks, global_blocks):
    q, keys, values = queries[0], keys_in[0], values_in[0]
    me = lax.axis_index("seq")
    early_heads = HEADS_KV - LATE
    cut = LATE * HEAD
    near_cols = slice(LATE * QW, (HEADS_KV - FAR) * QW)
    always = me >= 0

    first, high, far_a = opening(random_blocks.transpose(2, 0, 1), global_blocks[0], q, keys, values)
    high = along(high, "segment", 1)
    far_a = along(far_a, "segment", -1)

    def edges(*parts):
        last = jnp.concatenate([x[ROWS - BLOCK :] for x in parts], axis=1)
        leading = jnp.concatenate([x[:BLOCK] for x in parts], axis=1)
        return along(last, "seq", 1), along(leading, "seq", -1)

    def ask(first, q, blocks, listed):
        owners = blocks.reshape(BLOCKS * RAND) // BLOCKS
        row = jnp.concatenate([owners, jnp.zeros((HEAD - BLOCKS * RAND,), jnp.int32)]).astype(BF)
        holder = jnp.where(me < DEVS // GLOB, listed[:1], listed[1:]) // BLOCKS
        flags = jnp.stack([me > 0, me < DEVS - 1]).astype(jnp.int32)
        return (
            exchange(first), q[:, near_cols], q[:, (HEADS_KV - 1) * QW :],
            owners, jnp.broadcast_to(row[None], (PIECE, HEAD)), holder, flags, *edges(keys[:, :cut], values[:, :cut]),
        )

    def ask_shapes(q):
        ints = [jnp.zeros((n,), jnp.int32) for n in (BLOCKS * RAND, 1, 2)]
        return (
            jnp.zeros(first.shape, BF), q[:, near_cols], q[:, :QW],
            ints[0], jnp.zeros((PIECE, HEAD), BF), ints[1], ints[2],
            jnp.zeros((BLOCK, 2 * cut), BF), jnp.zeros((BLOCK, 2 * cut), BF),
        )

    def no_ask(first, q, blocks, listed):
        return jax.tree.map(lambda x: jnp.zeros(x.shape, x.dtype), jax.eval_shape(ask_shapes, q))

    message, near_q, far_b, owners, own_tile, holder, flags, before, after = lax.cond(
        always, ask, no_ask, first, q, random_blocks[0], global_blocks[0]
    )
    packed, notes = pack_first(holder, keys, values, message, own_tile)
    notes = along(notes, "segment", 1)
    packed, notes, far_a, high = lax.optimization_barrier((packed, notes, far_a, high))
    got = exchange(packed)
    near_q = along(tied(near_q, notes), "segment", 1)
    far_b = along(tied(far_b, notes), "segment", -1)
    far_a = along(tied(far_a, notes), "segment", -1)
    asked_at = notes.shape[0] - PIECE - DEVS
    asked_e = notes[asked_at:-PIECE, 0].astype(jnp.int32)
    owners_e = notes[-PIECE, : BLOCKS * RAND].astype(jnp.int32)

    before_e, after_e = edges(high)
    packed = pack(asked_e, [(high, c) for c in range(2 * early_heads)], notes[:asked_at])
    got_e = exchange(packed)

    sent = []
    slots = owners
    far_a = along(tied(far_a, got), "segment", -1)
    far_b = along(tied(far_b, got), "segment", -1)
    for h in range(LATE):
        if h == 1:
            slots, near_q, far_b = lax.optimization_barrier((slots, near_q, far_b))
        if h == 2:
            slots, far_a = lax.optimization_barrier((slots, far_a))
        res = attention(
            slots, flags, 1, h, [(q, h, 1)], keys, h, values, h, before, after, (h, LATE + h), got, 0, LATE
        )
        slots = tied(owners, res)
        sent.append(along(res, "segment", 1))
    far_b = along(far_b, "segment", -1)

    out = place(tied(sent[0], res), None, 0, q.shape[1])
    out = place(tied(sent[1], res), out, 1)
    parts = [(near_q, 0, early_heads - FAR), (far_a, 0, 1), (far_b, 0, 1)]
    out = attention(
        owners_e, flags, early_heads, LATE, parts, high, 0, high, early_heads, before_e, after_e,
        (0, early_heads), got_e, LATE, early_heads, width=q.shape[1], out=out,
    )
    out = place(sent[2], out, 2)
    return out[None]


def solution(mesh):
    in_specs = (
        P("segment", "seq", None),
        P("segment", "seq", None),
        P("segment", "seq", None),
        P("segment", "seq", None),
        P("segment", None),
    )
    out_specs = P("segment", "seq", None)
    return jax.shard_map(
        per_device, mesh=mesh, in_specs=in_specs, out_specs=out_specs, check_vma=False
    )
```

```python
import math

import jax
import jax.numpy as jnp
from jax import lax
from jax.experimental import pallas as pl
from jax.experimental.pallas import tpu as pltpu
from jax.sharding import PartitionSpec as P

HEAD = 128
BLOCK = 64
GLOB = 2
RAND = 3
ROWS = 512
BLOCKS = ROWS // BLOCK
GROUP = 8
HEADS_KV = 8
PAIRS = HEADS_KV // 2
LATE = 3
FAR = 2
DEVS = 32
PIECE = 16
KEYS = 512
WEIGHT = 20
QW = GROUP * HEAD
BF = jnp.bfloat16
SCALE = math.log2(math.e) / math.sqrt(HEAD)
VMEM_BYTES = 63 << 20
CHEAP = pl.CostEstimate(flops=0, bytes_accessed=0, transcendentals=0)


def attention_cost(heads):
    scores = heads * GROUP * ROWS * KEYS
    return pl.CostEstimate(
        flops=WEIGHT * 4 * scores * HEAD, bytes_accessed=WEIGHT * 4 * heads * ROWS * QW, transcendentals=scores
    )


def along(x, axis, by):
    n = lax.axis_size(axis)
    return lax.ppermute(x, axis, [(i, (i + by) % n) for i in range(n)])


def exchange(x):
    return lax.all_to_all(x, "seq", split_axis=0, concat_axis=0, tiled=True)


def params():
    return pltpu.CompilerParams(vmem_limit_bytes=VMEM_BYTES)


def opening(random_blocks, global_blocks, q, keys, values):
    cut = LATE * HEAD
    rest = keys.shape[1] - cut
    message_shape = (DEVS, (PAIRS + 1) * PIECE, HEAD)
    shapes = [message_shape, (ROWS, 2 * rest), (ROWS, QW)]

    def body(rb, gb, q_ref, k_ref, v_ref, out_hbm, high_hbm, far_hbm, out, high, far, glob, sems, glob_sems):
        base = lax.axis_index("seq") * BLOCKS
        globs = []
        for g in range(GLOB):
            at = jnp.minimum(jnp.maximum(gb[g] - base, 0), BLOCKS - 1) * BLOCK
            rows = pl.ds(pl.multiple_of(at, BLOCK), BLOCK)
            for n, src in enumerate((k_ref, v_ref)):
                globs.append(pltpu.make_async_copy(src.at[rows], glob.at[n, g], glob_sems.at[2 * n + g]))
        half = [pl.ds(i * ROWS // 2, ROWS // 2) for i in range(2)]
        high_loads, far_loads, high_stores, far_stores = [], [], [], []
        for i, rows in enumerate(half):
            high_loads += [
                pltpu.make_async_copy(
                    k_ref.at[rows, pl.ds(cut, rest)], high.at[rows, pl.ds(0, rest)], sems.at[i]
                ),
                pltpu.make_async_copy(
                    v_ref.at[rows, pl.ds(cut, rest)], high.at[rows, pl.ds(rest, rest)], sems.at[2 + i]
                ),
            ]
            far_loads.append(
                pltpu.make_async_copy(
                    q_ref.at[rows, pl.ds((HEADS_KV - FAR) * QW, QW)], far.at[rows], sems.at[4 + i]
                )
            )
            high_stores.append(pltpu.make_async_copy(high.at[rows], high_hbm.at[rows], sems.at[6 + i]))
            far_stores.append(pltpu.make_async_copy(far.at[rows], far_hbm.at[rows], sems.at[8 + i]))
        last_store = pltpu.make_async_copy(out, out_hbm, sems.at[10])
        for c in high_loads + far_loads + globs:
            c.start()
        out[:, PAIRS * PIECE :] = jnp.zeros((DEVS, PIECE, HEAD), BF)
        for r in range(RAND):
            for j in range(BLOCKS):
                wanted = rb[r, 0, j]
                out[lax.shift_right_logical(wanted, 3), PAIRS * PIECE :] = jnp.full(
                    (PIECE, HEAD), wanted & (BLOCKS - 1), jnp.int32
                ).astype(jnp.float32).astype(BF)
        for i in range(2):
            high_loads[2 * i].wait()
            high_loads[2 * i + 1].wait()
            high_stores[i].start()
        for i in range(2):
            far_loads[i].wait()
            far_stores[i].start()
        for c in globs:
            c.wait()
        for i in range(DEVS):
            g, t, part = i // 16, (i % 16) // 4, i % 4
            for c in range(PAIRS):
                head = 2 * c + t % 2
                out[i, c * PIECE : (c + 1) * PIECE] = glob[
                    t // 2, g, part * PIECE : (part + 1) * PIECE, head * HEAD : (head + 1) * HEAD
                ]
        last_store.start()
        for c in high_stores + far_stores + [last_store]:
            c.wait()

    here = pl.BlockSpec(memory_space=pltpu.HBM)
    return pl.pallas_call(
        body,
        grid_spec=pltpu.PrefetchScalarGridSpec(
            num_scalar_prefetch=2,
            grid=(1,),
            in_specs=[here] * 3,
            out_specs=[here] * 3,
            scratch_shapes=[pltpu.VMEM(x, BF) for x in shapes]
            + [
                pltpu.VMEM((2, GLOB, BLOCK, keys.shape[1]), BF),
                pltpu.SemaphoreType.DMA((11,)),
                pltpu.SemaphoreType.DMA((2 * GLOB,)),
            ],
        ),
        out_shape=[jax.ShapeDtypeStruct(x, BF) for x in shapes],
        compiler_params=params(),
        cost_estimate=CHEAP,
    )(random_blocks, global_blocks, q, keys, values)


def pack(asked, sources, pieces):
    step = 8
    arrays = []
    for x, _ in sources:
        if not any(x is y for y in arrays):
            arrays.append(x)
    tiles = [([x is y for y in arrays].index(True), at * HEAD) for x, at in sources]
    widths = [max(at for m, at in tiles if m == n) + HEAD for n in range(len(arrays))]
    extra = pieces.shape[0]
    slot_rows = len(tiles) * BLOCK + extra

    def body(ask, *refs):
        p_ref, out = refs[-2:]
        base = pl.program_id(0) * step
        for d in range(step):
            rows = pl.ds(pl.multiple_of(ask[base + d] * BLOCK, BLOCK), BLOCK)
            for t, (n, at) in enumerate(tiles):
                out[d, t * BLOCK : (t + 1) * BLOCK] = refs[n][rows, at : at + HEAD]
            out[d, len(tiles) * BLOCK :] = p_ref[...]

    def whole(*shape):
        return pl.BlockSpec(shape, lambda i, *_: (0, 0))

    return pl.pallas_call(
        body,
        grid_spec=pltpu.PrefetchScalarGridSpec(
            num_scalar_prefetch=1,
            grid=(DEVS // step,),
            in_specs=[whole(ROWS, w) for w in widths] + [whole(*pieces.shape)],
            out_specs=pl.BlockSpec((step, slot_rows, HEAD), lambda i, *_: (i, 0, 0)),
        ),
        out_shape=jax.ShapeDtypeStruct((DEVS, slot_rows, HEAD), BF),
        compiler_params=params(),
        cost_estimate=CHEAP,
    )(asked, *arrays, pieces)


def pack_first(holder, keys, values, message, owners):
    step = 8
    tiles = 2 * LATE
    cut = LATE * HEAD
    kept = (LATE + 1) // 2 * PIECE
    split = LATE // 2 * PIECE
    pieces = PAIRS * PIECE
    slot_rows = tiles * BLOCK + kept

    def body(held, k_ref, v_ref, ask_ref, p_ref, own_ref, out, notes):
        base = pl.program_id(0) * step
        ask = ask_ref[pl.ds(base, step), 0:1, :].astype(jnp.float32).astype(jnp.int32)
        for d in range(step):
            rows = pl.ds(pl.multiple_of(ask[d, 0, 0] * BLOCK, BLOCK), BLOCK)
            for t in range(tiles):
                src, at = (k_ref, v_ref)[t // LATE], t % LATE * HEAD
                out[d, t * BLOCK : (t + 1) * BLOCK] = src[rows, at : at + HEAD]
            out[d, tiles * BLOCK :] = p_ref[0, :kept]

        @pl.when(pl.program_id(0) == 0)
        def _():
            notes[: pieces - split] = p_ref[0, split:]
            notes[pieces - split : pieces - split + DEVS] = ask_ref[:, 0, :]
            notes[pieces - split + DEVS :] = own_ref[...]

    notes_rows = pieces - split + DEVS + PIECE
    return pl.pallas_call(
        body,
        grid_spec=pltpu.PrefetchScalarGridSpec(
            num_scalar_prefetch=1,
            grid=(DEVS // step,),
            in_specs=[
                pl.BlockSpec((ROWS, cut), lambda i, *_: (0, 0)),
                pl.BlockSpec((ROWS, cut), lambda i, *_: (0, 0)),
                pl.BlockSpec((DEVS, PIECE, HEAD), lambda i, *_: (0, PAIRS, 0)),
                pl.BlockSpec((1, pieces, HEAD), lambda i, held: (held[0], 0, 0)),
                pl.BlockSpec((PIECE, HEAD), lambda i, *_: (0, 0)),
            ],
            out_specs=[
                pl.BlockSpec((step, slot_rows, HEAD), lambda i, *_: (i, 0, 0)),
                pl.BlockSpec((notes_rows, HEAD), lambda i, *_: (0, 0)),
            ],
        ),
        out_shape=[
            jax.ShapeDtypeStruct((DEVS, slot_rows, HEAD), BF),
            jax.ShapeDtypeStruct((notes_rows, HEAD), BF),
        ],
        compiler_params=params(),
        cost_estimate=CHEAP,
    )(holder, keys, values, message, message, owners)


def attention(slots, flags, heads, first, qs, k, k_at, v, v_at, before, after, halo_at, got, got_first, got_heads, width=None, out=None):
    hk_at, hv_at = halo_at
    cuts = 1
    half = BLOCKS // cuts
    part_rows = half * BLOCK
    counts = [n for _, _, n in qs]
    starts = [sum(counts[:i]) for i in range(len(qs))]

    def body(slot, flag, *refs):
        q_refs = refs[: len(qs)]
        k_ref, v_ref, kb, vb, ka, va, rk, rv, gl, *rest = refs[len(qs) :]
        o_ref, kpad, vpad, kcat, vcat, *q_scratch = rest[-5 - (len(qs) > 1) :] if len(qs) > 1 else rest[-5:]
        h, part = pl.program_id(0), pl.program_id(1)
        if len(qs) > 1:
            q_ref = q_scratch[0]
            for i, some in enumerate(q_refs):
                @pl.when((h >= starts[i]) & (h < starts[i] + counts[i]))
                def _(some=some):
                    q_ref[...] = some[...]
        else:
            q_ref = q_refs[0]

        @pl.when(part == 0)
        def _():
            odd = lax.rem(first + h, 2)
            for pad, own, b, a in ((kpad, k_ref, kb, ka), (vpad, v_ref, vb, va)):
                pad[0:BLOCK] = b[...]
                pad[BLOCK : BLOCK + ROWS] = own[...]
                pad[BLOCK + ROWS :] = a[...]
            for buf in range(2):
                for g in range(GLOB):
                    for i in range(4):
                        at = 3 * BLOCK + g * BLOCK + i * PIECE
                        kcat[buf, at : at + PIECE] = gl[g * 16 + odd * 4 + i]
                        vcat[buf, at : at + PIECE, 0:HEAD] = gl[g * 16 + (2 + odd) * 4 + i]
                vcat[buf, :, HEAD:] = jnp.ones((KEYS, HEAD), BF)

        for j in range(half):
            buf = j % 2
            window = pl.ds(pl.multiple_of(part * part_rows + j * BLOCK, BLOCK), 3 * BLOCK)
            kcat[buf, 0 : 3 * BLOCK] = kpad[window]
            vcat[buf, 0 : 3 * BLOCK, 0:HEAD] = vpad[window]
            for r in range(RAND):
                s = slot[(part * half + j) * RAND + r]
                at = (3 + GLOB + r) * BLOCK
                kcat[buf, at : at + BLOCK] = rk[s]
                vcat[buf, at : at + BLOCK, 0:HEAD] = rv[s]
            rows = slice(j * BLOCK, (j + 1) * BLOCK)
            part_heads = 2
            for u in range(GROUP // part_heads):
                mine = range(u * part_heads, (u + 1) * part_heads)
                qq = jnp.concatenate([q_ref[rows, g * HEAD : (g + 1) * HEAD] for g in mine], axis=0)
                s = lax.dot_general(
                    qq, kcat[buf], (((1,), (1,)), ((), ())), preferred_element_type=jnp.float32
                )
                if j == 0 or j == half - 1:
                    col = lax.broadcasted_iota(jnp.int32, (1, KEYS), 1)
                    if j == 0:
                        hide = (col < BLOCK) & (flag[0] == 0) & (part == 0)
                    else:
                        hide = (col >= 2 * BLOCK) & (col < 3 * BLOCK) & (flag[1] == 0) & (part == cuts - 1)
                    s = jnp.where(hide, -jnp.inf, s)
                top = jnp.max(s, axis=-1, keepdims=True)
                e = jnp.exp2((s - top) * SCALE).astype(BF)
                o = lax.dot_general(
                    e, vcat[buf], (((1,), (0,)), ((), ())), preferred_element_type=jnp.float32
                )
                o = (o[:, :HEAD] / o[:, HEAD:]).astype(BF)
                for n, g in enumerate(mine):
                    o_ref[rows, g * HEAD : (g + 1) * HEAD] = o[n * BLOCK : (n + 1) * BLOCK]

    def col(shape, at):
        return pl.BlockSpec(shape, lambda h, *_: (0, at + h))

    def q_spec(i):
        _, at, n = qs[i]
        lo = starts[i]

        def index(h, p, *_):
            here = (h >= lo) & (h < lo + n)
            row = jnp.where(here, p, jnp.where(h < lo, 0, cuts - 1))
            return row, at + jnp.minimum(jnp.maximum(h - lo, 0), n - 1)

        return pl.BlockSpec((part_rows, QW), index)

    at = first - got_first
    glob_at = 2 * got_heads * BLOCK // PIECE - got_first // 2
    in_specs = [q_spec(i) for i in range(len(qs))] + [
        col((ROWS, HEAD), k_at),
        col((ROWS, HEAD), v_at),
        col((BLOCK, HEAD), hk_at),
        col((BLOCK, HEAD), hv_at),
        col((BLOCK, HEAD), hk_at),
        col((BLOCK, HEAD), hv_at),
        pl.BlockSpec((DEVS, BLOCK, HEAD), lambda h, *_: (0, at + h, 0)),
        pl.BlockSpec((DEVS, BLOCK, HEAD), lambda h, *_: (0, got_heads + at + h, 0)),
        pl.BlockSpec((DEVS, PIECE, HEAD), lambda h, *_: (0, glob_at + lax.div(first + h, 2), 0)),
    ]
    operands = [slots, flags, *[x for x, _, _ in qs], k, v, before, before, after, after, got, got, got]
    aliases = {}
    if out is not None:
        in_specs.append(pl.BlockSpec(memory_space=pl.ANY))
        aliases = {len(operands): 0}
        operands.append(out)
    out_at = first if width else 0
    scratch = [
        pltpu.VMEM((ROWS + 2 * BLOCK, HEAD), BF),
        pltpu.VMEM((ROWS + 2 * BLOCK, HEAD), BF),
        pltpu.VMEM((2, KEYS, HEAD), BF),
        pltpu.VMEM((2, KEYS, 2 * HEAD), BF),
    ]
    if len(qs) > 1:
        scratch.append(pltpu.VMEM((part_rows, QW), BF))
    return pl.pallas_call(
        body,
        grid_spec=pltpu.PrefetchScalarGridSpec(
            num_scalar_prefetch=2,
            grid=(heads, cuts),
            in_specs=in_specs,
            out_specs=pl.BlockSpec((part_rows, QW), lambda h, p, *_: (p, out_at + h)),
            scratch_shapes=scratch,
        ),
        out_shape=jax.ShapeDtypeStruct((ROWS, width or heads * QW), BF),
        input_output_aliases=aliases,
        compiler_params=params(),
        cost_estimate=attention_cost(heads),
    )(*operands)


def place(part, out, at, width=None):
    cuts = 8
    step = ROWS // cuts

    def body(p_ref, *refs):
        o_ref, stage, load_sems, store_sems = refs[-4:]
        loads, stores = [], []
        for i in range(cuts):
            rows = pl.ds(i * step, step)
            loads.append(pltpu.make_async_copy(p_ref.at[rows], stage.at[rows], load_sems.at[i]))
            stores.append(
                pltpu.make_async_copy(stage.at[rows], o_ref.at[rows, pl.ds(at * QW, QW)], store_sems.at[i])
            )
        for c in loads:
            c.start()
        for x, y in zip(loads, stores):
            x.wait()
            y.start()
        for c in stores:
            c.wait()

    here = pl.BlockSpec(memory_space=pltpu.HBM)
    operands = [part]
    if out is not None:
        operands.append(out)
        width = out.shape[1]
    return pl.pallas_call(
        body,
        in_specs=[here] * len(operands),
        out_specs=here,
        out_shape=jax.ShapeDtypeStruct((ROWS, width), BF),
        scratch_shapes=[
            pltpu.VMEM((ROWS, QW), BF),
            pltpu.SemaphoreType.DMA((cuts,)),
            pltpu.SemaphoreType.DMA((cuts,)),
        ],
        input_output_aliases={} if out is None else {1: 0},
        compiler_params=params(),
        cost_estimate=CHEAP,
    )(*operands)


def tied(x, *others):
    return lax.optimization_barrier((x, *others))[0]


def per_device(queries, keys_in, values_in, random_blocks, global_blocks):
    q, keys, values = queries[0], keys_in[0], values_in[0]
    me = lax.axis_index("seq")
    early_heads = HEADS_KV - LATE
    cut = LATE * HEAD
    near_cols = slice(LATE * QW, (HEADS_KV - FAR) * QW)
    always = me >= 0

    first, high, far_a = opening(random_blocks.transpose(2, 0, 1), global_blocks[0], q, keys, values)
    high = along(high, "segment", 1)
    far_a = along(far_a, "segment", -1)

    def edges(*parts):
        last = jnp.concatenate([x[ROWS - BLOCK :] for x in parts], axis=1)
        leading = jnp.concatenate([x[:BLOCK] for x in parts], axis=1)
        return along(last, "seq", 1), along(leading, "seq", -1)

    def ask(first, q, blocks, listed):
        owners = blocks.reshape(BLOCKS * RAND) // BLOCKS
        row = jnp.concatenate([owners, jnp.zeros((HEAD - BLOCKS * RAND,), jnp.int32)]).astype(BF)
        holder = jnp.where(me < DEVS // GLOB, listed[:1], listed[1:]) // BLOCKS
        flags = jnp.stack([me > 0, me < DEVS - 1]).astype(jnp.int32)
        return (
            exchange(first),
            owners, jnp.broadcast_to(row[None], (PIECE, HEAD)), holder, flags, *edges(keys[:, :cut], values[:, :cut]),
        )

    def ask_shapes(q):
        ints = [jnp.zeros((n,), jnp.int32) for n in (BLOCKS * RAND, 1, 2)]
        return (
            jnp.zeros(first.shape, BF),
            ints[0], jnp.zeros((PIECE, HEAD), BF), ints[1], ints[2],
            jnp.zeros((BLOCK, 2 * cut), BF), jnp.zeros((BLOCK, 2 * cut), BF),
        )

    def no_ask(first, q, blocks, listed):
        return jax.tree.map(lambda x: jnp.zeros(x.shape, x.dtype), jax.eval_shape(ask_shapes, q))

    message, owners, own_tile, holder, flags, before, after = lax.cond(
        always, ask, no_ask, first, q, random_blocks[0], global_blocks[0]
    )
    packed, notes = pack_first(holder, keys, values, message, own_tile)
    notes = along(notes, "segment", 1)
    near_q, far_b = q[:, near_cols], q[:, (HEADS_KV - 1) * QW :]
    packed, notes, far_a, high, near_q, far_b = lax.optimization_barrier(
        (packed, notes, far_a, high, near_q, far_b)
    )
    got = exchange(packed)
    near_q = along(tied(near_q, notes), "segment", 1)
    far_b = along(tied(far_b, notes), "segment", -1)
    far_a = along(tied(far_a, notes), "segment", -1)
    asked_at = notes.shape[0] - PIECE - DEVS
    asked_e = notes[asked_at:-PIECE, 0].astype(jnp.int32)
    owners_e = notes[-PIECE, : BLOCKS * RAND].astype(jnp.int32)

    before_e, after_e = edges(high)
    packed = pack(asked_e, [(high, c) for c in range(2 * early_heads)], notes[:asked_at])
    got_e = exchange(packed)

    sent = []
    slots = owners
    far_a = along(tied(far_a, got), "segment", -1)
    far_b = along(tied(far_b, got), "segment", -1)
    for h in range(LATE):
        if h == 1:
            slots, near_q, far_b = lax.optimization_barrier((slots, near_q, far_b))
        if h == 2:
            slots, far_a = lax.optimization_barrier((slots, far_a))
        res = attention(
            slots, flags, 1, h, [(q, h, 1)], keys, h, values, h, before, after, (h, LATE + h), got, 0, LATE
        )
        slots = tied(owners, res)
        sent.append(along(res, "segment", 1))
    far_b = along(far_b, "segment", -1)

    out = place(tied(sent[0], res), None, 0, q.shape[1])
    out = place(tied(sent[1], res), out, 1)
    parts = [(near_q, 0, early_heads - FAR), (far_a, 0, 1), (far_b, 0, 1)]
    out = attention(
        owners_e, flags, early_heads, LATE, parts, high, 0, high, early_heads, before_e, after_e,
        (0, early_heads), got_e, LATE, early_heads, width=q.shape[1], out=out,
    )
    out = place(sent[2], out, 2)
    return out[None]


def solution(mesh):
    in_specs = (
        P("segment", "seq", None),
        P("segment", "seq", None),
        P("segment", "seq", None),
        P("segment", "seq", None),
        P("segment", None),
    )
    out_specs = P("segment", "seq", None)
    return jax.shard_map(
        per_device, mesh=mesh, in_specs=in_specs, out_specs=out_specs, check_vma=False
    )
```
